256 devices in a mesh: row: 8 (over z_hi, y), col: 32 (over x, z_lo, core).
Axes of the slice: x: 4, y: 4, z: 8 (z_hi: 2, z_lo: 4; z = z_hi * 4 + z_lo), core: 2. Of those that a mesh axis runs over, the one named last changes fastest.
Arguments:
- row_feats: bfloat16 [64, 8192], P(None, ('row', 'col')), may hold values from -0.75 to 0.75
- row_alpha: bfloat16 [8192], P(('row', 'col')), may hold values from -18 to 18
- row_solves: bfloat16 [32, 8192], P(None, ('row', 'col')), may hold values from -288 to 288
- col_feats: bfloat16 [64, 262144], P('row', 'col'), may hold values from -0.75 to 0.75
- col_alpha: bfloat16 [262144], P('col'), may hold values from -18 to 18
- col_weight: float32 [262144], P('col'), may hold values from 0.02 to 0.25
- col_probes: bfloat16 [32, 262144], P('row', 'col'), may hold values from -6 to 6
Outputs:
- grad_rows: float32 [64, 8192], P(None, ('row', 'col'))
- grad_cols: float32 [64, 262144], P('row', 'col')
The draws below stay inside these ranges and needn't reach their ends.
All inputs are finite; a program needn't handle non-finite values.
Results may differ from the reference program's by a relative error of at most 0.0075.
Values may be sent and summed in bfloat16 or wider, within the bound.
A program may use at most 64 MiB of HBM per device.

```python
import math
import jax
import jax.numpy as jnp
from jax import lax

FEAT = 64
PROBES = 32
COL_DEV = 8192
WIN = 8192
NPTS = 262144


def block_levels(rng, dims, split, low, high):
    def one(axis_at, parts):
        heights = jax.random.uniform(jax.random.fold_in(jax.random.fold_in(rng, 6), axis_at), (parts,), jnp.float32, low / len(split), high / len(split))
        return jnp.repeat(jnp.exp(heights), dims[axis_at] // parts).reshape((-1,) + (1,) * (len(dims) - axis_at - 1))

    loudness = one(*split[0])
    for cut in split[1:]:
        loudness = loudness * one(*cut)
    return loudness


def noise(key, extent, spread, most, pieces=(), held_as=jnp.bfloat16):
    level = block_levels(key, extent, pieces, -0.22, 0.18) if pieces else 1.0
    values = jax.random.normal(key, extent, jnp.float32) * spread * level
    return jnp.minimum(jnp.maximum(values, -most), most).astype(held_as)


def setup_inputs(seed: int = 0) -> dict:
    streams_of = jax.random.split(jax.random.key(seed), 8)
    row_feats = noise(streams_of[0], (FEAT, WIN), 0.125, 0.75, ((1, 256),))
    row_alpha = noise(streams_of[1], (WIN,), 3.0, 18.0, ((0, 256),))
    row_solves = noise(streams_of[2], (PROBES, WIN), 48.0, 288.0, ((1, 256),))
    col_feats = noise(streams_of[3], (FEAT, NPTS), 0.125, 0.75, ((0, 8), (1, 32)))
    col_alpha = noise(streams_of[4], (NPTS,), 3.0, 18.0, ((0, 32),))
    col_weight = jnp.clip(jnp.exp(math.log(0.25) - 2.5257287 * jax.random.uniform(streams_of[5], (NPTS,), jnp.float32) ** block_levels(streams_of[5], (NPTS,), ((0, 32),), -0.2, 0.2)), 0.02, 0.25)
    col_probes = noise(streams_of[6], (PROBES, NPTS), 1.0, 6.0, ((0, 8), (1, 32)))
    return dict(row_feats=row_feats, row_alpha=row_alpha, row_solves=row_solves, col_feats=col_feats, col_alpha=col_alpha, col_weight=col_weight, col_probes=col_probes)


def tile_terms(row_feats, left, sq_row, col_feats, right, sq_col):
    contract = (((0,), (0,)), ((), ()))
    cross = lax.dot_general(row_feats, col_feats, contract, preferred_element_type=jnp.float32)
    kernel = jnp.exp(-(sq_row[:, None] + sq_col[None, :] - 2.0 * cross) * 0.5)
    weight = lax.dot_general(left, right, contract, preferred_element_type=jnp.float32)
    product = (weight * kernel).astype(jnp.bfloat16)
    row_sum = jnp.sum(product.astype(jnp.float32), axis=1)
    col_sum = jnp.sum(product.astype(jnp.float32), axis=0)
    toward_row = lax.dot_general(col_feats, product, (((1,), (1,)), ((), ())), preferred_element_type=jnp.float32)
    toward_col = jnp.dot(row_feats, product, preferred_element_type=jnp.float32)
    part_row = toward_row - row_sum[None, :] * row_feats.astype(jnp.float32)
    part_col = toward_col - col_sum[None, :] * col_feats.astype(jnp.float32)
    return part_row, part_col


def reference(row_feats, row_alpha, row_solves, col_feats, col_alpha, col_weight, col_probes):
    left = jnp.concatenate([row_alpha[None, :], row_solves], axis=0)
    sq_row = jnp.sum(jnp.square(row_feats.astype(jnp.float32)), axis=0)
    probe_part = (-0.5 / PROBES) * col_weight[None, :] * col_probes.astype(jnp.float32)
    right = jnp.concatenate([0.5 * col_alpha.astype(jnp.float32)[None, :], probe_part], axis=0).astype(jnp.bfloat16)
    sq_col = jnp.sum(jnp.square(col_feats.astype(jnp.float32)), axis=0)
    blocks = NPTS // COL_DEV

    def one_block(step, carry):
        total_row, total_col = carry
        start = (step * COL_DEV)
        feats = lax.dynamic_slice_in_dim(col_feats, start, COL_DEV, 1)
        rights = lax.dynamic_slice_in_dim(right, start, COL_DEV, 1)
        squares = lax.dynamic_slice_in_dim(sq_col, start, COL_DEV, 0)
        part_row, part_col = tile_terms(row_feats, left, sq_row, feats, rights, squares)
        total_col = lax.dynamic_update_slice_in_dim(total_col, part_col, start, 1)
        return total_row + part_row, total_col

    start_row = jnp.zeros((FEAT, WIN), jnp.float32)
    start_col = jnp.zeros((FEAT, NPTS), jnp.float32)
    total_row, total_col = lax.fori_loop(0, blocks, one_block, (start_row, start_col))
    grad_rows = total_row * (1.0 / (NPTS ** 0.5))
    grad_cols = total_col * (1.0 / (WIN ** 0.5))
    return grad_rows, grad_cols
```

```python
import functools

import jax
import jax.numpy as jnp
from jax import lax
from jax.experimental import pallas as pl
from jax.experimental.pallas import tpu as pltpu
from jax.sharding import PartitionSpec as P

MESH = pl.DeviceIdType.MESH
F32 = jnp.float32
BF16 = jnp.bfloat16

FEAT = 64
PROBES = 32
NX, NY, NZ = 4, 4, 8
TILE = 1024
ITEM = 512

ORDER = (
    (0, 0, 0), (0, 0, 1), (0, 1, 0),
    (1, 0, 0), (1, 0, 1), (1, 1, 0), (1, 1, 1),
    (3, 0, 0), (3, 0, 1), (3, 1, 0), (3, 1, 1),
    (2, 0, 0), (2, 0, 1), (2, 1, 0), (2, 1, 1),
    (0, 1, 1),
)


def look(values, at):
    out = jnp.int32(values[0])
    for k, v in enumerate(values[1:], 1):
        out = jnp.where(at == k, jnp.int32(v), out)
    return out


def parts3(v):
    hi = v.astype(BF16).astype(F32)
    mid = (v - hi).astype(BF16).astype(F32)
    return hi, mid, v - hi - mid


def kernel(
    row_scale, col_scale,
    rf_ref, ra_ref, rs_ref, cf_ref, ca_ref, cw_ref, cp_ref,
    out_rows, out_cols,
    rows, send_cols, recv_cols, cx, cr, xct, acc_col, acc_row, part, got,
    y_out, y_in, z_out, z_in, back_out, back_in,
    col_s, col_r, z_s, z_r, y_s, y_r, g_s, g_r, f_s,
    part_s, part_r, yy_s, yy_r, zz_s, zz_r, back_s, back_r,
):
    row = lax.axis_index("row")
    col = lax.axis_index("col")
    y, core = row % 4, col % 2
    x, z = col // 8, (row // 4) * 4 + (col // 2) % 4

    def at(px, py, pz, pc):
        return {"row": (pz // 4) * 4 + py, "col": (px * 4 + pz % 4) * 2 + pc}

    def z_peer(d):
        return at(x, y, (z + d) % NZ, core)

    def y_peer(d):
        return at(x, (y + d) % NY, z, core)

    def row_peer(d):
        return {"row": (row + d) % 8, "col": col}

    barrier = pltpu.get_barrier_semaphore()
    peers = [z_peer(d) for d in range(1, NZ)] + [y_peer(d) for d in range(1, NY)]
    peers += [at((x + d) % NX, y, z, core) for d in range(1, NX)]
    peers += [at((x + d) % NX, y, z, 1 - core) for d in range(NX)]
    peers += [at(x, (y + d) % NY, (z + 4) % NZ, core) for d in range(1, NY)]
    for peer in peers:
        pl.semaphore_signal(barrier, inc=1, device_id=peer, device_id_type=MESH)

    rf = rf_ref[...].astype(F32)
    n = rf.shape[1]
    sq = -0.5 * jnp.sum(rf * rf, axis=0, keepdims=True)
    one = jnp.ones((1, n), F32)
    mine = jnp.concatenate(
        [rf, one, one, one, *parts3(sq), ra_ref[...].astype(F32), jnp.zeros((1, n), F32),
         rs_ref[...].astype(F32), jnp.zeros((24, n), F32)], axis=0)
    mine = jnp.concatenate([mine, jnp.zeros((128, 128 - n), F32)], axis=1)
    me_g = x * 2 + core
    rows[me_g, y, z] = mine.T[:n].astype(BF16)

    for p in range(8):
        feats = cf_ref[:, p * TILE:(p + 1) * TILE].astype(F32)
        probes = cp_ref[:, p * TILE:(p + 1) * TILE].astype(F32)
        left = jnp.concatenate([feats[:, :512], feats[:, 512:]], axis=0)
        right = jnp.concatenate([probes[:, q * 256:(q + 1) * 256] for q in range(4)], axis=0)
        send_cols[p] = jnp.concatenate([left, right], axis=1).astype(BF16)

    pl.semaphore_wait(barrier, len(peers))

    def z_copy(d):
        return pltpu.make_async_remote_copy(
            src_ref=rows.at[me_g, y, z], dst_ref=rows.at[me_g, y, z],
            send_sem=z_s.at[d], recv_sem=z_r.at[d], device_id=z_peer(d), device_id_type=MESH)

    def col_copy(d):
        return pltpu.make_async_remote_copy(
            src_ref=send_cols.at[(row + d) % 8], dst_ref=recv_cols.at[row],
            send_sem=col_s.at[d], recv_sem=col_r.at[d], device_id=row_peer(d), device_id_type=MESH)

    def y_copy(d):
        return pltpu.make_async_remote_copy(
            src_ref=rows.at[me_g, y], dst_ref=rows.at[me_g, y],
            send_sem=y_s.at[d], recv_sem=y_r.at[d], device_id=y_peer(d), device_id_type=MESH)

    def g_copy(g, d, peer, send_sem):
        return pltpu.make_async_remote_copy(
            src_ref=rows.at[g], dst_ref=rows.at[g],
            send_sem=send_sem.at[d], recv_sem=g_r.at[g], device_id=peer, device_id_type=MESH)

    def x_copy(d):
        return g_copy(me_g, d, at((x + d) % NX, y, z, core), g_s)

    def core_copy(g, d):
        return g_copy(g, d, at(x, y, z, 1 - core), f_s)

    z_copies = [z_copy(d) for d in range(1, NZ)]
    for c in z_copies:
        c.start()
    col_copies = [col_copy(d) for d in range(1, 8)]
    for c in col_copies:
        c.start()
    recv_cols[row] = send_cols[row]
    for c in z_copies:
        c.wait_recv()
    y_copies = [y_copy(d) for d in range(1, NY)]
    for c in y_copies:
        c.start()
    for c in y_copies:
        c.wait_recv()
    x_copies = [x_copy(d) for d in (1, 3, 2)] + [core_copy(me_g, 0)]
    for c in x_copies:
        c.start()
    for c in col_copies:
        c.wait_recv()

    feats = jnp.concatenate(
        [jnp.concatenate([recv_cols[p, 0:16, 0:512].astype(F32)[8 * h:8 * h + 8] for h in range(2)], axis=1)
         for p in range(8)], axis=0)
    probes = []
    for p in range(8):
        block = recv_cols[p, 0:16, 512:768].astype(F32)
        probes.append(jnp.concatenate([block[4 * q:4 * q + 4] for q in range(4)], axis=1))
    probes = jnp.concatenate(probes, axis=0)
    mask = lax.broadcasted_iota(jnp.int32, (8, TILE), 0) == row
    weight = jnp.sum(jnp.where(mask, cw_ref[...], 0.0), axis=0, keepdims=True)
    alpha = jnp.sum(jnp.where(mask, ca_ref[...].astype(F32), 0.0), axis=0, keepdims=True)
    sq = -0.5 * jnp.sum(feats * feats, axis=0, keepdims=True)
    one = jnp.ones((1, TILE), F32)
    none = jnp.zeros((1, TILE), F32)
    cx[...] = jnp.concatenate(
        [feats, *parts3(sq), one, one, one, none, none, jnp.zeros((56, TILE), F32)], axis=0).astype(BF16)
    cr[...] = jnp.concatenate(
        [jnp.zeros((70, TILE), F32), 0.5 * alpha, none, (-0.5 / PROBES) * weight * probes,
         jnp.zeros((24, TILE), F32)], axis=0).astype(BF16)
    xct[...] = jnp.concatenate(
        [feats, one, jnp.zeros((63, TILE), F32)], axis=0).T.astype(BF16)

    acc_col[...] = jnp.zeros_like(acc_col)
    lane = lax.broadcasted_iota(jnp.int32, (ITEM // 2, 128), 1)

    def part_copy(s, dx, dc):
        return pltpu.make_async_remote_copy(
            src_ref=part.at[s], dst_ref=got.at[s], send_sem=part_s.at[s], recv_sem=part_r.at[s],
            device_id=at((x + dx) % NX, y, z, (core + dc) % 2), device_id_type=MESH)

    def item(s, _):
        dx = look([o[0] for o in ORDER], s)
        dc = look([o[1] for o in ORDER], s)
        half = look([o[2] for o in ORDER], s)
        first = jnp.logical_and(s >= 2, jnp.logical_and(half == 0, True))
        g = ((x + dx) % NX) * 2 + (core + dc) % 2

        @pl.when(first)
        def _():
            core_copy(g, 0).wait_recv()

        @pl.when(jnp.logical_and(first, dc == 0))
        def _():
            core_copy(g, dx).start()

        r = rows[g, pl.ds(half * 2, 2)].reshape(ITEM, 128)
        cross = jnp.dot(r, cx[...], preferred_element_type=F32)
        weights = jnp.dot(r, cr[...], preferred_element_type=F32)
        prod = (weights * jnp.exp(cross)).astype(BF16)
        t = jnp.dot(prod, xct[...], preferred_element_type=F32)
        acc_col[...] += jnp.dot(r.T[0:80], prod, preferred_element_type=F32)
        t = t - t[:, 64:65] * r.astype(F32)
        t = t.reshape(ITEM // 32, 2, 16, 128)
        lo = t[:, 0].reshape(ITEM // 2, 128)
        hi = t[:, 1].reshape(ITEM // 2, 128)
        packed = jnp.where(lane < 64, lo, pltpu.roll(hi, 64, axis=1))

        @pl.when(s < 2)
        def _():
            acc_row[half] = packed

        @pl.when(s >= 2)
        def _():
            part[s] = packed.astype(BF16)
            part_copy(s, dx, dc).start()

        return 0

    lax.fori_loop(0, len(ORDER), item, 0)

    grad = (acc_col[0:64] - acc_col[64:65] * cx[0:64].astype(F32)) * col_scale
    for p in range(8):
        block = grad[8 * p:8 * p + 8]
        back_out[p] = jnp.concatenate([block[:, :512], block[:, 512:]], axis=0).astype(BF16)

    def back_copy(d):
        return pltpu.make_async_remote_copy(
            src_ref=back_out.at[(row + d) % 8], dst_ref=back_in.at[row],
            send_sem=back_s.at[d], recv_sem=back_r.at[d], device_id=row_peer(d), device_id_type=MESH)

    back_copies = [back_copy(d) for d in range(1, 8)]
    for c in back_copies:
        c.start()
    back_in[row] = back_out[row]

    for s in range(2, len(ORDER)):
        part_copy(s, *ORDER[s][:2]).wait_recv()
    for h in range(2):
        total = acc_row[h]
        for s in range(2, len(ORDER)):
            if ORDER[s][2] == h:
                total += got[s].astype(F32)
        acc_row[h] = total
        y_out[2 * h:2 * h + 2] = total.reshape(2, 128, 128).astype(BF16)

    def yy_copy(d):
        return pltpu.make_async_remote_copy(
            src_ref=y_out.at[(y + d) % NY], dst_ref=y_in.at[d],
            send_sem=yy_s.at[d], recv_sem=yy_r.at[d], device_id=y_peer(d), device_id_type=MESH)

    yy_copies = [yy_copy(d) for d in range(1, NY)]
    for c in yy_copies:
        c.start()
    total = acc_row[y // 2, pl.ds(pl.multiple_of((y % 2) * 128, 128), 128)]
    for c, d in zip(yy_copies, range(1, NY)):
        c.wait_recv()
        total += y_in[d].astype(F32)
    z_out[...] = total.reshape(NZ, 16, 128).astype(BF16)

    def zz_copy(d):
        return pltpu.make_async_remote_copy(
            src_ref=z_out.at[(z + d) % NZ], dst_ref=z_in.at[d],
            send_sem=zz_s.at[d], recv_sem=zz_r.at[d], device_id=z_peer(d), device_id_type=MESH)

    zz_copies = [zz_copy(d) for d in range(1, NZ)]
    for c in zz_copies:
        c.start()
    total = z_out[z].astype(F32)
    for c, d in zip(zz_copies, range(1, NZ)):
        c.wait_recv()
        total += z_in[d].astype(F32)
    total = total * row_scale
    final = jnp.concatenate([total, pltpu.roll(total, 64, axis=1), jnp.zeros((96, 128), F32)], axis=0)
    out_rows[...] = final.T[0:64, 0:32]

    for c in back_copies:
        c.wait_recv()
    for p in range(8):
        block = back_in[p].astype(F32)
        out_cols[:, p * TILE:p * TILE + 512] = block[0:8]
        out_cols[:, p * TILE + 512:(p + 1) * TILE] = block[8:16]

    for c in z_copies + col_copies + y_copies + x_copies + back_copies + yy_copies + zz_copies:
        c.wait_send()
    for d in range(1, NX):
        core_copy(((x + d) % NX) * 2 + core, d).wait_send()
    for s in range(2, len(ORDER)):
        part_copy(s, *ORDER[s][:2]).wait_send()


def body(row_feats, row_alpha, row_solves, col_feats, col_alpha, col_weight, col_probes):
    row_size = lax.axis_size("row")
    col_size = lax.axis_size("col")
    window = row_alpha.shape[0] * row_size * col_size
    points = col_alpha.shape[0] * col_size
    dma = pltpu.SemaphoreType.DMA
    vmem = pl.BlockSpec(memory_space=pltpu.VMEM)
    items = len(ORDER)
    return pl.pallas_call(
        functools.partial(kernel, 1.0 / points**0.5, 1.0 / window**0.5),
        out_shape=(
            jax.ShapeDtypeStruct((FEAT, row_feats.shape[1]), F32),
            jax.ShapeDtypeStruct((FEAT // row_size, col_feats.shape[1]), F32),
        ),
        in_specs=[vmem] * 7,
        out_specs=(vmem, vmem),
        scratch_shapes=[
            pltpu.VMEM((2 * NX, NY, NZ, 32, 128), BF16),
            pltpu.VMEM((8, 16, 768), BF16),
            pltpu.VMEM((8, 16, 768), BF16),
            pltpu.VMEM((128, TILE), BF16),
            pltpu.VMEM((128, TILE), BF16),
            pltpu.VMEM((TILE, 128), BF16),
            pltpu.VMEM((80, TILE), F32),
            pltpu.VMEM((2, ITEM // 2, 128), F32),
            pltpu.VMEM((items, ITEM // 2, 128), BF16),
            pltpu.VMEM((items, ITEM // 2, 128), BF16),
            pltpu.VMEM((NY, 128, 128), BF16),
            pltpu.VMEM((NY, 128, 128), BF16),
            pltpu.VMEM((NZ, 16, 128), BF16),
            pltpu.VMEM((NZ, 16, 128), BF16),
            pltpu.VMEM((8, 16, 512), BF16),
            pltpu.VMEM((8, 16, 512), BF16),
            dma((8,)), dma((8,)), dma((NZ,)), dma((NZ,)), dma((NY,)), dma((NY,)),
            dma((NX,)), dma((2 * NX,)), dma((NX,)),
            dma((items,)), dma((items,)), dma((NY,)), dma((NY,)), dma((NZ,)), dma((NZ,)),
            dma((8,)), dma((8,)),
        ],
        compiler_params=pltpu.CompilerParams(
            collective_id=0, has_side_effects=True, vmem_limit_bytes=48 * 2**20),
        name="evidence_gradients",
    )(
        row_feats, row_alpha.reshape(1, -1), row_solves, col_feats,
        col_alpha.reshape(row_size, -1), col_weight.reshape(row_size, -1), col_probes,
    )


def solution(mesh):
    in_specs = (
        P(None, ("row", "col")),
        P(("row", "col")),
        P(None, ("row", "col")),
        P("row", "col"),
        P("col"),
        P("col"),
        P("row", "col"),
    )
    out_specs = (P(None, ("row", "col")), P("row", "col"))
    return jax.shard_map(body, mesh=mesh, in_specs=in_specs, out_specs=out_specs, check_vma=False)
```

```python
import functools

import jax
import jax.numpy as jnp
from jax import lax
from jax.experimental import pallas as pl
from jax.experimental.pallas import tpu as pltpu
from jax.sharding import PartitionSpec as P

MESH = pl.DeviceIdType.MESH
F32 = jnp.float32
BF16 = jnp.bfloat16

FEAT = 64
PROBES = 32
NX, NY, NZ = 4, 4, 8
TILE = 1024
ITEM = 512
HALF = 16

ORDER = (
    ((0, 0), (1, 0), (1, 1), (3, 0), (3, 1), (2, 0), (2, 1), (0, 1)),
    ((0, 1), (1, 0), (1, 1), (3, 0), (3, 1), (2, 0), (2, 1), (0, 0)),
)
ITEMS = 16
F8 = jnp.float8_e4m3fn
UP = 512.0
LOG2E = 1.4426950408889634


def look(values, at):
    out = jnp.int32(values[0])
    for k, v in enumerate(values[1:], 1):
        out = jnp.where(at == k, jnp.int32(v), out)
    return out


def lookup(s, k):
    flat = [ORDER[i % 2][i // 2][k] for i in range(ITEMS)]
    return look(flat, s)


def split8(v):
    hi = v.astype(F8).astype(F32)
    return hi, (v - hi).astype(F8).astype(F32)


def parts3(v):
    hi = v.astype(BF16).astype(F32)
    mid = (v - hi).astype(BF16).astype(F32)
    return hi, mid, v - hi - mid


def kernel(
    row_scale, col_scale,
    rf_hbm, ra_hbm, rs_hbm, cf_hbm, ca_hbm, cw_hbm, cp_hbm,
    out_rows, out_cols,
    rf_ref, ra_ref, rs_ref, cf_ref, ca_ref, cw_ref, cp_ref, in_s,
    zbuf, rows, send_cols, recv_cols, relay, cx, cf8, cb, cr, xct, small, acc_col,
    keep, core_out, core_in, axis_out, axis_in,
    mid_out, mid_in, z_out, z_in, back_out, back_in, back_relay,
    col_s, col_r, z_s, z_r, m_s, m_r, g_s, g_r, f_s,
    core_s, core_r, axis_s, axis_r, mm_s, mm_r, zz_s, zz_r, back_s, back_r,
):
    row = lax.axis_index("row")
    col = lax.axis_index("col")
    y, core = row % 4, col % 2
    x, z = col // 8, (row // 4) * 4 + (col // 2) % 4

    def at(px, py, pz, pc):
        return {"row": (pz // 4) * 4 + py, "col": (px * 4 + pz % 4) * 2 + pc}

    def z_peer(d):
        return at(x, y, (z + d) % NZ, core)

    def axis_peer(t, d):
        return at((x + jnp.where(t == 0, d, 0)) % NX, (y + jnp.where(t == 1, d, 0)) % NY, z, core)

    sibling = at(x, y, z, 1 - core)
    far = (row + 4) % 8

    def row_of(d, other):
        return ((row // 4 + other) % 2) * 4 + (y + d) % 4

    def exchange(out, into, through, send, recv):
        def over_z(d):
            return pltpu.make_async_remote_copy(
                src_ref=out.at[row_of(d, 1)], dst_ref=through.at[d] if d else into.at[row],
                send_sem=send.at[0, d], recv_sem=recv.at[0, d], device_id=z_peer(4), device_id_type=MESH)

        def over_y(d):
            return pltpu.make_async_remote_copy(
                src_ref=out.at[row_of(d, 0)], dst_ref=into.at[row],
                send_sem=send.at[1, d], recv_sem=recv.at[1, d], device_id=axis_peer(1, d), device_id_type=MESH)

        def onward(d):
            return pltpu.make_async_remote_copy(
                src_ref=through.at[d], dst_ref=into.at[far],
                send_sem=send.at[2, d], recv_sem=recv.at[2, d], device_id=axis_peer(1, d), device_id_type=MESH)

        first = [over_z(d) for d in (2, 1, 3, 0)]
        second = [over_y(d) for d in (2, 1, 3)]
        third = [onward(d) for d in (2, 1, 3)]

        def start():
            for c in first + second:
                c.start()
            into[row] = out[row]

        def forward():
            for a, b in zip(first, third):
                a.wait_recv()
                b.start()

        def finish():
            for c in second + [first[3]] + third:
                c.wait_recv()

        def sent():
            for c in first + second + third:
                c.wait_send()

        return start, forward, finish, sent

    loads = [
        pltpu.make_async_copy(src, dst, in_s.at[k])
        for k, (src, dst) in enumerate((
            (rf_hbm, rf_ref), (ra_hbm, ra_ref), (rs_hbm, rs_ref), (cf_hbm, cf_ref),
            (cp_hbm, cp_ref), (ca_hbm, ca_ref), (cw_hbm, cw_ref)))
    ]
    for c in loads:
        c.start()

    barrier = pltpu.get_barrier_semaphore()
    peers = [z_peer(d) for d in range(1, NZ)] + [sibling]
    peers += [axis_peer(t, d) for t in range(2) for d in range(1, 4)]
    for peer in peers:
        pl.semaphore_signal(barrier, inc=1, device_id=peer, device_id_type=MESH)

    for c in loads[:3]:
        c.wait()
    n = 2 * HALF
    rf = rf_ref[...].astype(F32)
    sq = -0.5 * jnp.sum(rf * rf, axis=1, keepdims=True)
    at8 = lax.broadcasted_iota(jnp.int32, (8, n), 0)
    side = jnp.concatenate(
        [jnp.zeros((64, n), F32), jnp.where(at8 == 6, ra_ref[...].astype(F32), 0.0),
         rs_ref[...].astype(F32), jnp.zeros((24, n), F32)], axis=0)
    side = jnp.concatenate([side, jnp.zeros((128, 128 - n), F32)], axis=1).T[:n]
    lane = lax.broadcasted_iota(jnp.int32, (n, 128), 1)
    mine = side + jnp.concatenate([rf, jnp.zeros((n, 64), F32)], axis=1)
    mine = jnp.where(jnp.logical_and(lane >= 64, lane < 67), 1.0, mine)
    for k, v in enumerate(parts3(sq)):
        mine = jnp.where(lane == 67 + k, v, mine)
    zbuf[z] = mine.astype(BF16)

    for c in loads[3:5]:
        c.wait()
    for p in range(8):
        feats = cf_ref[:, p * TILE:(p + 1) * TILE].astype(F32)
        probes = cp_ref[:, p * TILE:(p + 1) * TILE].astype(F32)
        left = jnp.concatenate([feats[:, :512], feats[:, 512:]], axis=0)
        right = jnp.concatenate([probes[:, q * 256:(q + 1) * 256] for q in range(4)], axis=0)
        send_cols[p] = jnp.concatenate([left, right], axis=1).astype(BF16)

    pl.semaphore_wait(barrier, len(peers))

    def z_copy(d):
        return pltpu.make_async_remote_copy(
            src_ref=zbuf.at[z], dst_ref=zbuf.at[z],
            send_sem=z_s.at[d], recv_sem=z_r.at[d], device_id=z_peer(d), device_id_type=MESH)

    own = (x * 2 + core, y * 2 + core)
    place = (y, x)

    def m_copy(t, d):
        return pltpu.make_async_remote_copy(
            src_ref=rows.at[t, own[t], place[t]], dst_ref=rows.at[t, own[t], place[t]],
            send_sem=m_s.at[t, d], recv_sem=m_r.at[t, d], device_id=axis_peer(1 - t, d), device_id_type=MESH)

    def g_copy(t, g, peer, send_sem):
        return pltpu.make_async_remote_copy(
            src_ref=rows.at[t, g], dst_ref=rows.at[t, g],
            send_sem=send_sem, recv_sem=g_r.at[t, g], device_id=peer, device_id_type=MESH)

    def group(t, d, dc):
        return jnp.where(t == 0, (x + d) % NX, (y + d) % NY) * 2 + (core + dc) % 2

    def axis_copy(t, d):
        return g_copy(t, group(t, 0, 0), axis_peer(t, d), g_s.at[t, d])

    def sibling_copy(t, d):
        return g_copy(t, group(t, d, 0), sibling, f_s.at[t, d])

    z_copies = [z_copy(d) for d in range(1, NZ)]
    for c in z_copies:
        c.start()
    col_start, col_forward, col_finish, col_sent = exchange(send_cols, recv_cols, relay, col_s, col_r)
    col_start()
    for c in z_copies:
        c.wait_recv()
    m_copies = []
    for t in range(2):
        rows[t, own[t], place[t]] = zbuf[:, t * HALF:(t + 1) * HALF]
        m_copies.append([m_copy(t, d) for d in range(1, 4)])
        for c in m_copies[t]:
            c.start()
    col_forward()
    for t in range(2):
        for c in m_copies[t]:
            c.wait_recv()
        sibling_copy(t, 0).start()
        axis_copy(t, 1).start()
        axis_copy(t, 3).start()
    col_finish()

    feats = jnp.concatenate(
        [jnp.concatenate([recv_cols[p, :, 0:512].astype(F32)[8 * h:8 * h + 8] for h in range(2)], axis=1)
         for p in range(8)], axis=0)
    probes = []
    for p in range(8):
        block = recv_cols[p, :, 512:768].astype(F32)
        probes.append(jnp.concatenate([block[4 * q:4 * q + 4] for q in range(4)], axis=1))
    probes = jnp.concatenate(probes, axis=0)
    for c in loads[5:]:
        c.wait()
    eight = pl.ds(pl.multiple_of(row * 8, 8), 8)
    weight = cw_ref[eight, :]
    small[...] = ca_ref[...].astype(F32)
    alpha = small[eight, :]
    weight = jnp.concatenate([weight[k:k + 1] for k in range(8)], axis=1)
    alpha = jnp.concatenate([alpha[k:k + 1] for k in range(8)], axis=1)
    cb[...] = (-0.5 * LOG2E) * jnp.sum(feats * feats, axis=0, keepdims=True)
    cx[...] = feats.astype(BF16)
    hi, lo = split8(feats * UP)
    cf8[...] = jnp.concatenate([hi, lo, lo, hi], axis=0).astype(F8)
    at8 = lax.broadcasted_iota(jnp.int32, (8, TILE), 0)
    cr[...] = jnp.concatenate(
        [jnp.zeros((64, TILE), F32), jnp.where(at8 == 6, 0.5 * alpha, 0.0), (-0.5 / PROBES) * weight * probes,
         jnp.zeros((24, TILE), F32)], axis=0).astype(BF16)
    xct[...] = jnp.concatenate(
        [feats, jnp.where(at8 == 0, 1.0, 0.0), jnp.zeros((56, TILE), F32)], axis=0).T.astype(BF16)

    acc_col[...] = jnp.zeros_like(acc_col)
    lane = lax.broadcasted_iota(jnp.int32, (ITEM, 128), 1)

    def core_copy(t, d):
        return pltpu.make_async_remote_copy(
            src_ref=core_out.at[t, d], dst_ref=core_in.at[t, d],
            send_sem=core_s.at[t, d], recv_sem=core_r.at[t, d], device_id=sibling, device_id_type=MESH)

    def part_copy(t, d):
        return pltpu.make_async_remote_copy(
            src_ref=axis_out.at[t, d], dst_ref=axis_in.at[t, d],
            send_sem=axis_s.at[t, d], recv_sem=axis_r.at[t, d], device_id=axis_peer(t, d), device_id_type=MESH)

    def item(s, _):
        t = s % 2
        d, dc = lookup(s, 0), lookup(s, 1)
        borrowed = jnp.logical_and(s != 0, s != ITEMS - 1)
        g = group(t, d, dc)

        @pl.when(borrowed)
        def _():
            g_copy(t, g, sibling, f_s.at[t, 0]).wait_recv()

        @pl.when(jnp.logical_and(dc == 0, borrowed))
        def _():
            sibling_copy(t, d).start()

        @pl.when(jnp.logical_and(d == 1, dc == 0))
        def _():
            axis_copy(t, 2).start()

        r = rows[t, g].reshape(ITEM, 128)
        wide = r.astype(F32)
        hi, lo = split8(jnp.where(lane < 64, wide * UP, 0.0))
        both = jnp.where(lane < 64, hi, pltpu.roll(lo, 64, axis=1)).astype(F8)
        squares = jnp.where(jnp.logical_and(lane >= 67, lane < 70), wide * LOG2E, 0.0)
        squares = jnp.sum(squares, axis=1, keepdims=True)
        cross = jnp.dot(jnp.concatenate([both, both], axis=1), cf8[...], preferred_element_type=F32)
        weights = jnp.dot(r, cr[...], preferred_element_type=F32)
        prod = (weights * jnp.exp2(cross * (LOG2E / UP**2) + cb[...] + squares)).astype(BF16)
        out = jnp.dot(prod, xct[...], preferred_element_type=F32)
        acc_col[...] += jnp.dot(r.T[0:80], prod, preferred_element_type=F32)
        out = out - out[:, 64:65] * wide
        out = out.reshape(ITEM // HALF, 2, 8, 128)
        lo = out[:, 0].reshape(ITEM // 2, 128)
        hi = out[:, 1].reshape(ITEM // 2, 128)
        packed = jnp.where(lane[:ITEM // 2] < 64, lo, pltpu.roll(hi, 64, axis=1))

        @pl.when(dc == 0)
        def _():
            keep[t, d] = packed

        @pl.when(dc == 1)
        def _():
            core_out[t, d] = packed.astype(BF16)
            core_copy(t, d).start()

        before = 1 - t
        bd, bdc = lookup(s - 1, 0), lookup(s - 1, 1)

        @pl.when(jnp.logical_and(bdc == 1, bd != 0))
        def _():
            core_copy(before, bd).wait_recv()
            axis_out[before, bd] = (keep[before, bd] + core_in[before, bd].astype(F32)).astype(BF16)
            part_copy(before, bd).start()

        return 0

    lax.fori_loop(0, ITEMS, item, 0)

    grad = (acc_col[0:64] - acc_col[64:65] * cx[0:64].astype(F32)) * col_scale
    for p in range(8):
        block = grad[8 * p:8 * p + 8]
        back_out[p] = jnp.concatenate([block[:, :512], block[:, 512:]], axis=0).astype(BF16)

    back_start, back_forward, back_finish, back_sent = exchange(back_out, back_in, back_relay, back_s, back_r)
    back_start()

    def mm_copy(t, d):
        return pltpu.make_async_remote_copy(
            src_ref=mid_out.at[t, (place[t] + d) % 4], dst_ref=mid_in.at[t, d],
            send_sem=mm_s.at[t, d], recv_sem=mm_r.at[t, d], device_id=axis_peer(1 - t, d), device_id_type=MESH)

    mm_copies = []
    for t in range(2):
        core_copy(t, 0).wait_recv()
        total = keep[t, 0] + core_in[t, 0].astype(F32)
        for d in range(1, 4):
            part_copy(t, d).wait_recv()
            total += axis_in[t, d].astype(F32)
        keep[t, 0] = total
        mid_out[t] = total.reshape(4, 64, 128).astype(BF16)
        mm_copies.append([mm_copy(t, d) for d in range(1, 4)])
        for c in mm_copies[t]:
            c.start()
    back_forward()
    halves = []
    for t in range(2):
        total = keep[t, 0, pl.ds(pl.multiple_of(place[t] * 64, 64), 64), :]
        for c, d in zip(mm_copies[t], range(1, 4)):
            c.wait_recv()
            total += mid_in[t, d].astype(F32)
        halves.append(total.reshape(NZ, 8, 128))
    z_out[...] = jnp.concatenate(halves, axis=1).astype(BF16)

    def zz_copy(d):
        return pltpu.make_async_remote_copy(
            src_ref=z_out.at[(z + d) % NZ], dst_ref=z_in.at[d],
            send_sem=zz_s.at[d], recv_sem=zz_r.at[d], device_id=z_peer(d), device_id_type=MESH)

    zz_copies = [zz_copy(d) for d in range(1, NZ)]
    for c in zz_copies:
        c.start()
    total = z_out[z].astype(F32)
    for c, d in zip(zz_copies, range(1, NZ)):
        c.wait_recv()
        total += z_in[d].astype(F32)
    total = total * row_scale
    moved = pltpu.roll(total, 64, axis=1)
    final = jnp.concatenate([total[0:8], moved[0:8], total[8:16], moved[8:16]], axis=0)
    out_rows[...] = final[:, 0:64]

    back_finish()
    for p in range(8):
        block = back_in[p].astype(F32)
        out_cols[:, p * TILE:p * TILE + 512] = block[0:8]
        out_cols[:, p * TILE + 512:(p + 1) * TILE] = block[8:16]

    col_sent()
    back_sent()
    for c in z_copies + m_copies[0] + m_copies[1] + mm_copies[0] + mm_copies[1] + zz_copies:
        c.wait_send()
    for t in range(2):
        for d in range(4):
            sibling_copy(t, d).wait_send()
            core_copy(t, d).wait_send()
            if d:
                axis_copy(t, d).wait_send()
                part_copy(t, d).wait_send()


def body(row_feats, row_alpha, row_solves, col_feats, col_alpha, col_weight, col_probes):
    row_size = lax.axis_size("row")
    col_size = lax.axis_size("col")
    own_rows = row_alpha.shape[0]
    own_cols = col_alpha.shape[0]
    window = own_rows * row_size * col_size
    points = own_cols * col_size
    dma = pltpu.SemaphoreType.DMA
    vmem = pl.BlockSpec(memory_space=pltpu.VMEM)
    hbm = pl.BlockSpec(memory_space=pltpu.HBM)
    args = (
        row_feats.T, row_alpha.reshape(1, -1), row_solves, col_feats,
        col_alpha.reshape(-1, 128), col_weight.reshape(-1, 128), col_probes,
    )
    half = ITEM // 2
    grad_rows, grad_cols = pl.pallas_call(
        functools.partial(kernel, 1.0 / points**0.5, 1.0 / window**0.5),
        out_shape=(
            jax.ShapeDtypeStruct((own_rows, FEAT), F32),
            jax.ShapeDtypeStruct((FEAT // row_size, own_cols), F32),
        ),
        in_specs=[hbm] * 7,
        out_specs=(vmem, vmem),
        scratch_shapes=[
            *[pltpu.VMEM(a.shape, a.dtype) for a in args],
            dma((7,)),
            pltpu.VMEM((NZ, 2 * HALF, 128), BF16),
            pltpu.VMEM((2, 8, 4, NZ, HALF, 128), BF16),
            pltpu.VMEM((8, 16, 768), BF16),
            pltpu.VMEM((8, 16, 768), BF16),
            pltpu.VMEM((4, 16, 768), BF16),
            pltpu.VMEM((FEAT, TILE), BF16),
            pltpu.VMEM((4 * FEAT, TILE), F8),
            pltpu.VMEM((1, TILE), F32),
            pltpu.VMEM((128, TILE), BF16),
            pltpu.VMEM((TILE, 128), BF16),
            pltpu.VMEM((own_cols // 128, 128), F32),
            pltpu.VMEM((80, TILE), F32),
            pltpu.VMEM((2, 4, half, 128), F32),
            *[pltpu.VMEM((2, 4, half, 128), BF16)] * 4,
            *[pltpu.VMEM((2, 4, half // 4, 128), BF16)] * 2,
            *[pltpu.VMEM((NZ, 16, 128), BF16)] * 2,
            *[pltpu.VMEM((8, 16, 512), BF16)] * 2,
            pltpu.VMEM((4, 16, 512), BF16),
            dma((3, 4)), dma((3, 4)), dma((NZ,)), dma((NZ,)), dma((2, 4)), dma((2, 4)),
            dma((2, 4)), dma((2, 8)), dma((2, 4)),
            *[dma((2, 4))] * 6,
            dma((NZ,)), dma((NZ,)), dma((3, 4)), dma((3, 4)),
        ],
        compiler_params=pltpu.CompilerParams(
            collective_id=0, has_side_effects=True, vmem_limit_bytes=63 * 2**20),
        name="evidence_gradients",
    )(*args)
    return grad_rows.T, grad_cols


def solution(mesh):
    in_specs = (
        P(None, ("row", "col")),
        P(("row", "col")),
        P(None, ("row", "col")),
        P("row", "col"),
        P("col"),
        P("col"),
        P("row", "col"),
    )
    out_specs = (P(None, ("row", "col")), P("row", "col"))
    return jax.shard_map(body, mesh=mesh, in_specs=in_specs, out_specs=out_specs, check_vma=False)
```

```python
import functools

import jax
import jax.numpy as jnp
from jax import lax
from jax.experimental import pallas as pl
from jax.experimental.pallas import tpu as pltpu
from jax.sharding import PartitionSpec as P

MESH = pl.DeviceIdType.MESH
F32 = jnp.float32
BF16 = jnp.bfloat16

FEAT = 64
PROBES = 32
NX, NY, NZ = 4, 4, 8
TILE = 1024
ITEM = 512
HALF = 16

ORDER = ((0, 1), (1, 0), (1, 1), (3, 1), (3, 0), (2, 1), (2, 0), (0, 0))
PASS_ON = (0, 1, 3, 0, 2, 0, 0, 0)
ADD_UP = (0, 0, 0, 1, 3, 0, 2, 0)


def look(values, at):
    out = jnp.int32(values[0])
    for k, v in enumerate(values[1:], 1):
        out = jnp.where(at == k, jnp.int32(v), out)
    return out


def parts3(v):
    hi = v.astype(BF16).astype(F32)
    mid = (v - hi).astype(BF16).astype(F32)
    return hi, mid, v - hi - mid


def kernel(
    row_scale, col_scale,
    rf_hbm, ra_hbm, rs_hbm, cf_hbm, ca_hbm, cw_hbm, cp_hbm,
    out_rows, out_cols,
    rf_ref, ra_ref, rs_ref, cf_ref, ca_ref, cw_ref, cp_ref, in_s,
    zbuf, rows, send_cols, recv_cols, relay, cx, cr, xct, small, acc_col,
    keep, core_out, core_in, axis_out, axis_in,
    mid_out, mid_in, z_out, z_in, back_out, back_in, back_relay,
    col_s, col_r, z_s, z_r, m_s, m_r, g_s, g_r, f_s,
    core_s, core_r, axis_s, axis_r, mm_s, mm_r, zz_s, zz_r, back_s, back_r,
):
    row = lax.axis_index("row")
    col = lax.axis_index("col")
    y, core = row % 4, col % 2
    x, z = col // 8, (row // 4) * 4 + (col // 2) % 4

    def at(px, py, pz, pc):
        return {"row": (pz // 4) * 4 + py, "col": (px * 4 + pz % 4) * 2 + pc}

    def z_peer(d):
        return at(x, y, (z + d) % NZ, core)

    def axis_peer(t, d):
        return at((x + jnp.where(t == 0, d, 0)) % NX, (y + jnp.where(t == 1, d, 0)) % NY, z, core)

    sibling = at(x, y, z, 1 - core)
    far = (row + 4) % 8

    def row_of(d, other):
        return ((row // 4 + other) % 2) * 4 + (y + d) % 4

    def exchange(out, into, through, send, recv):
        def over_z(d):
            return pltpu.make_async_remote_copy(
                src_ref=out.at[row_of(d, 1)], dst_ref=through.at[d] if d else into.at[row],
                send_sem=send.at[0, d], recv_sem=recv.at[0, d], device_id=z_peer(4), device_id_type=MESH)

        def over_y(d):
            return pltpu.make_async_remote_copy(
                src_ref=out.at[row_of(d, 0)], dst_ref=into.at[row],
                send_sem=send.at[1, d], recv_sem=recv.at[1, d], device_id=axis_peer(1, d), device_id_type=MESH)

        def onward(d):
            return pltpu.make_async_remote_copy(
                src_ref=through.at[d], dst_ref=into.at[far],
                send_sem=send.at[2, d], recv_sem=recv.at[2, d], device_id=axis_peer(1, d), device_id_type=MESH)

        first = [over_z(d) for d in (2, 1, 3, 0)]
        second = [over_y(d) for d in (2, 1, 3)]
        third = [onward(d) for d in (2, 1, 3)]

        def start():
            for c in first + second:
                c.start()
            into[row] = out[row]

        def forward():
            for a, b in zip(first, third):
                a.wait_recv()
                b.start()

        def finish():
            for c in second + [first[3]] + third:
                c.wait_recv()

        def sent():
            for c in first + second + third:
                c.wait_send()

        return start, forward, finish, sent

    loads = [
        pltpu.make_async_copy(src, dst, in_s.at[k])
        for k, (src, dst) in enumerate((
            (rf_hbm, rf_ref), (ra_hbm, ra_ref), (rs_hbm, rs_ref), (cf_hbm, cf_ref),
            (cp_hbm, cp_ref), (ca_hbm, ca_ref), (cw_hbm, cw_ref)))
    ]
    for c in loads:
        c.start()

    barrier = pltpu.get_barrier_semaphore()
    peers = [z_peer(d) for d in range(1, NZ)] + [sibling]
    peers += [axis_peer(t, d) for t in range(2) for d in range(1, 4)]
    for peer in peers:
        pl.semaphore_signal(barrier, inc=1, device_id=peer, device_id_type=MESH)

    for c in loads[:3]:
        c.wait()
    n = 2 * HALF
    rf = rf_ref[...].astype(F32)
    sq = -0.5 * jnp.sum(rf * rf, axis=1, keepdims=True)
    at8 = lax.broadcasted_iota(jnp.int32, (8, n), 0)
    side = jnp.concatenate(
        [jnp.zeros((64, n), F32), jnp.where(at8 == 6, ra_ref[...].astype(F32), 0.0),
         rs_ref[...].astype(F32), jnp.zeros((24, n), F32)], axis=0)
    side = jnp.concatenate([side, jnp.zeros((128, 128 - n), F32)], axis=1).T[:n]
    lane = lax.broadcasted_iota(jnp.int32, (n, 128), 1)
    mine = side + jnp.concatenate([rf, jnp.zeros((n, 64), F32)], axis=1)
    mine = jnp.where(jnp.logical_and(lane >= 64, lane < 67), 1.0, mine)
    for k, v in enumerate(parts3(sq)):
        mine = jnp.where(lane == 67 + k, v, mine)
    zbuf[z] = mine.astype(BF16)

    for c in loads[3:5]:
        c.wait()
    for p in range(8):
        span = slice(p * TILE, (p + 1) * TILE)
        feats = cf_ref[:, span].astype(F32)
        probes = cp_ref[:, span].astype(F32)
        left = jnp.concatenate([feats[:, :512], feats[:, 512:]], axis=0)
        right = jnp.concatenate([probes[:, q * 256:(q + 1) * 256] for q in range(4)], axis=0)
        send_cols[p] = jnp.concatenate([left, right], axis=1).astype(BF16)

    for c in loads[5:]:
        c.wait()
    eight = pl.ds(pl.multiple_of(row * 8, 8), 8)
    weight = cw_ref[eight, :]
    small[...] = ca_ref[...].astype(F32)
    alpha = small[eight, :]
    weight = jnp.concatenate([weight[k:k + 1] for k in range(8)], axis=1) * (-0.5 / PROBES)
    alpha = jnp.concatenate([alpha[k:k + 1] for k in range(8)], axis=1) * 0.5
    xct[:, 128:] = jnp.ones((TILE, 128), BF16)
    acc_col[...] = jnp.zeros_like(acc_col)

    pl.semaphore_wait(barrier, len(peers))

    def z_copy(d):
        return pltpu.make_async_remote_copy(
            src_ref=zbuf.at[z], dst_ref=zbuf.at[z],
            send_sem=z_s.at[d], recv_sem=z_r.at[d], device_id=z_peer(d), device_id_type=MESH)

    own = (x * 2 + core, y * 2 + core)
    place = (y, x)

    def m_copy(t, d):
        return pltpu.make_async_remote_copy(
            src_ref=rows.at[t, own[t], place[t]], dst_ref=rows.at[t, own[t], place[t]],
            send_sem=m_s.at[t, d], recv_sem=m_r.at[t, d], device_id=axis_peer(1 - t, d), device_id_type=MESH)

    def g_copy(t, g, peer, send_sem):
        return pltpu.make_async_remote_copy(
            src_ref=rows.at[t, g], dst_ref=rows.at[t, g],
            send_sem=send_sem, recv_sem=g_r.at[t, g], device_id=peer, device_id_type=MESH)

    def group(t, d, dc):
        return jnp.where(t == 0, (x + d) % NX, (y + d) % NY) * 2 + (core + dc) % 2

    def axis_copy(t, d):
        return g_copy(t, group(t, 0, 0), axis_peer(t, d), g_s.at[t, d])

    def sibling_copy(t, d):
        return g_copy(t, group(t, d, 0), sibling, f_s.at[t, d])

    z_copies = [z_copy(d) for d in range(1, NZ)]
    for c in z_copies:
        c.start()
    col_start, col_forward, col_finish, col_sent = exchange(send_cols, recv_cols, relay, col_s, col_r)
    col_start()
    for c in z_copies:
        c.wait_recv()
    m_copies = []
    for t in range(2):
        rows[t, own[t], place[t]] = zbuf[:, t * HALF:(t + 1) * HALF]
        m_copies.append([m_copy(t, d) for d in range(1, 4)])
        for c in m_copies[t]:
            c.start()
    col_forward()
    for t in range(2):
        for c in m_copies[t]:
            c.wait_recv()
        sibling_copy(t, 0).start()
        axis_copy(t, 1).start()
        axis_copy(t, 3).start()
    col_finish()

    feats = jnp.concatenate(
        [jnp.concatenate([recv_cols[p, :, 0:512].astype(F32)[8 * k:8 * k + 8] for k in range(2)], axis=1)
         for p in range(8)], axis=0)
    probes = []
    for p in range(8):
        block = recv_cols[p, :, 512:768].astype(F32)
        probes.append(jnp.concatenate([block[4 * q:4 * q + 4] for q in range(4)], axis=1))
    probes = jnp.concatenate(probes, axis=0)
    sq = parts3(-0.5 * jnp.sum(feats * feats, axis=0, keepdims=True))
    at8 = lax.broadcasted_iota(jnp.int32, (8, TILE), 0)
    side = jnp.where(at8 < 6, 1.0, 0.0)
    for k, v in enumerate(sq):
        side = jnp.where(at8 == k, v, side)
    cx[...] = jnp.concatenate([feats, side, jnp.zeros((56, TILE), F32)], axis=0).astype(BF16)
    cr[...] = jnp.concatenate(
        [jnp.zeros((64, TILE), F32), jnp.where(at8 == 6, alpha, 0.0), weight * probes,
         jnp.zeros((24, TILE), F32)], axis=0).astype(BF16)
    xct[:, 0:128] = jnp.concatenate([feats, feats], axis=0).T.astype(BF16)

    low = lax.broadcasted_iota(jnp.int32, (ITEM, 128), 1) < 64

    def groups(g0, g1):
        return jnp.concatenate([rows[0, g0].reshape(ITEM, 128), rows[1, g1].reshape(ITEM, 128)], axis=0)

    def products(r):
        cross = jnp.dot(r, cx[...], preferred_element_type=F32)
        weights = jnp.dot(r, cr[...], preferred_element_type=F32)
        prod = (weights * jnp.exp(cross)).astype(BF16)
        out = jnp.dot(prod, xct[...], preferred_element_type=F32)
        acc_col[...] += jnp.dot(r.T[0:80], prod, preferred_element_type=F32)
        return out

    def pack(out, r):
        def pick(v, k):
            return v.reshape(2 * ITEM // HALF, 2, 8, 128)[:, k].reshape(ITEM, 128)

        wide = r.astype(F32)
        feats = jnp.where(low, pick(wide, 0), pltpu.roll(pick(wide, 1), 64, axis=1))
        toward, total = out[:, :128], out[:, 128:]
        return (jnp.where(low, pick(toward, 0), pick(toward, 1))
                - jnp.where(low, pick(total, 0), pick(total, 1)) * feats)

    def core_copy(t, d):
        return pltpu.make_async_remote_copy(
            src_ref=core_out.at[t, d], dst_ref=core_in.at[t, d],
            send_sem=core_s.at[t, d], recv_sem=core_r.at[t, d], device_id=sibling, device_id_type=MESH)

    def part_copy(t, d):
        return pltpu.make_async_remote_copy(
            src_ref=axis_out.at[t, d], dst_ref=axis_in.at[t, d],
            send_sem=axis_s.at[t, d], recv_sem=axis_r.at[t, d], device_id=axis_peer(t, d), device_id_type=MESH)

    def begin(d, dc, passed):
        for t in range(2):
            @pl.when(passed != 0)
            def _():
                g_copy(t, group(t, passed, 0), sibling, f_s.at[t, 0]).wait_recv()
                sibling_copy(t, passed).start()

            @pl.when(dc == 1)
            def _():
                g_copy(t, group(t, d, 1), sibling, f_s.at[t, 0]).wait_recv()

    def end(packed, d, dc, added):
        half = ITEM // 2

        @pl.when(dc == 0)
        def _():
            for t in range(2):
                keep[t, d] = packed[t * half:(t + 1) * half]

        @pl.when(dc == 1)
        def _():
            for t in range(2):
                core_out[t, d] = packed[t * half:(t + 1) * half].astype(BF16)
                core_copy(t, d).start()

        @pl.when(added != 0)
        def _():
            for t in range(2):
                core_copy(t, added).wait_recv()
                axis_out[t, added] = (keep[t, added] + core_in[t, added].astype(F32)).astype(BF16)
                part_copy(t, added).start()

    def step(s, _):
        d, dc = look([o[0] for o in ORDER], s), look([o[1] for o in ORDER], s)

        @pl.when(s == 1)
        def _():
            for t in range(2):
                axis_copy(t, 2).start()

        begin(d, dc, look(PASS_ON, s))
        r = groups(group(0, d, dc), group(1, d, dc))
        end(pack(products(r), r), d, dc, look(ADD_UP, s))
        return 0

    lax.fori_loop(0, len(ORDER), step, 0)

    grad = (acc_col[0:64] - acc_col[64:65] * cx[0:64].astype(F32)) * col_scale
    for p in range(8):
        block = grad[8 * p:8 * p + 8]
        back_out[p] = jnp.concatenate([block[:, :512], block[:, 512:]], axis=0).astype(BF16)
    back_start, back_forward, back_finish, back_sent = exchange(back_out, back_in, back_relay, back_s, back_r)
    back_start()

    def mm_copy(t, d):
        return pltpu.make_async_remote_copy(
            src_ref=mid_out.at[t, (place[t] + d) % 4], dst_ref=mid_in.at[t, d],
            send_sem=mm_s.at[t, d], recv_sem=mm_r.at[t, d], device_id=axis_peer(1 - t, d), device_id_type=MESH)

    mm_copies = []
    for t in range(2):
        core_copy(t, 0).wait_recv()
        total = keep[t, 0] + core_in[t, 0].astype(F32)
        for d in range(1, 4):
            part_copy(t, d).wait_recv()
            total += axis_in[t, d].astype(F32)
        keep[t, 0] = total
        mid_out[t] = total.reshape(4, 64, 128).astype(BF16)
        mm_copies.append([mm_copy(t, d) for d in range(1, 4)])
        for c in mm_copies[t]:
            c.start()
    back_forward()
    blocks = []
    for t in range(2):
        total = keep[t, 0, pl.ds(pl.multiple_of(place[t] * 64, 64), 64), :]
        for c, d in zip(mm_copies[t], range(1, 4)):
            c.wait_recv()
            total += mid_in[t, d].astype(F32)
        blocks.append(total.reshape(NZ, 8, 128))
    z_out[...] = jnp.concatenate(blocks, axis=1).astype(BF16)

    def zz_copy(d):
        return pltpu.make_async_remote_copy(
            src_ref=z_out.at[(z + d) % NZ], dst_ref=z_in.at[d],
            send_sem=zz_s.at[d], recv_sem=zz_r.at[d], device_id=z_peer(d), device_id_type=MESH)

    zz_copies = [zz_copy(d) for d in range(1, NZ)]
    for c in zz_copies:
        c.start()
    total = z_out[z].astype(F32)
    for c, d in zip(zz_copies, range(1, NZ)):
        c.wait_recv()
        total += z_in[d].astype(F32)
    total = total * row_scale
    moved = pltpu.roll(total, 64, axis=1)
    final = jnp.concatenate([total[0:8], moved[0:8], total[8:16], moved[8:16]], axis=0)
    out_rows[...] = final[:, 0:64]

    back_finish()
    for p in range(8):
        block = back_in[p].astype(F32)
        out_cols[:, p * TILE:p * TILE + 512] = block[0:8]
        out_cols[:, p * TILE + 512:(p + 1) * TILE] = block[8:16]

    col_sent()
    back_sent()
    for c in z_copies + m_copies[0] + m_copies[1] + mm_copies[0] + mm_copies[1] + zz_copies:
        c.wait_send()
    for t in range(2):
        for d in range(4):
            sibling_copy(t, d).wait_send()
            core_copy(t, d).wait_send()
            if d:
                axis_copy(t, d).wait_send()
                part_copy(t, d).wait_send()


def body(row_feats, row_alpha, row_solves, col_feats, col_alpha, col_weight, col_probes):
    row_size = lax.axis_size("row")
    col_size = lax.axis_size("col")
    own_rows = row_alpha.shape[0]
    own_cols = col_alpha.shape[0]
    window = own_rows * row_size * col_size
    points = own_cols * col_size
    dma = pltpu.SemaphoreType.DMA
    vmem = pl.BlockSpec(memory_space=pltpu.VMEM)
    hbm = pl.BlockSpec(memory_space=pltpu.HBM)
    args = (
        row_feats.T, row_alpha.reshape(1, -1), row_solves, col_feats,
        col_alpha.reshape(-1, 128), col_weight.reshape(-1, 128), col_probes,
    )
    half = ITEM // 2
    grad_rows, grad_cols = pl.pallas_call(
        functools.partial(kernel, 1.0 / points**0.5, 1.0 / window**0.5),
        out_shape=(
            jax.ShapeDtypeStruct((own_rows, FEAT), F32),
            jax.ShapeDtypeStruct((FEAT // row_size, own_cols), F32),
        ),
        in_specs=[hbm] * 7,
        out_specs=(vmem, vmem),
        scratch_shapes=[
            *[pltpu.VMEM(a.shape, a.dtype) for a in args],
            dma((7,)),
            pltpu.VMEM((NZ, 2 * HALF, 128), BF16),
            pltpu.VMEM((2, 8, 4, NZ, HALF, 128), BF16),
            pltpu.VMEM((8, 16, 768), BF16),
            pltpu.VMEM((8, 16, 768), BF16),
            pltpu.VMEM((4, 16, 768), BF16),
            pltpu.VMEM((128, TILE), BF16),
            pltpu.VMEM((128, TILE), BF16),
            pltpu.VMEM((TILE, 256), BF16),
            pltpu.VMEM((own_cols // 128, 128), F32),
            pltpu.VMEM((80, TILE), F32),
            pltpu.VMEM((2, 4, half, 128), F32),
            *[pltpu.VMEM((2, 4, half, 128), BF16)] * 4,
            *[pltpu.VMEM((2, 4, half // 4, 128), BF16)] * 2,
            *[pltpu.VMEM((NZ, 16, 128), BF16)] * 2,
            *[pltpu.VMEM((8, 16, 512), BF16)] * 2,
            pltpu.VMEM((4, 16, 512), BF16),
            dma((3, 4)), dma((3, 4)), dma((NZ,)), dma((NZ,)), dma((2, 4)), dma((2, 4)),
            dma((2, 4)), dma((2, 8)), dma((2, 4)),
            *[dma((2, 4))] * 6,
            dma((NZ,)), dma((NZ,)), dma((3, 4)), dma((3, 4)),
        ],
        compiler_params=pltpu.CompilerParams(
            collective_id=0, has_side_effects=True, vmem_limit_bytes=63 * 2**20),
        name="evidence_gradients",
    )(*args)
    return grad_rows.T, grad_cols


def solution(mesh):
    in_specs = (
        P(None, ("row", "col")),
        P(("row", "col")),
        P(None, ("row", "col")),
        P("row", "col"),
        P("col"),
        P("col"),
        P("row", "col"),
    )
    out_specs = (P(None, ("row", "col")), P("row", "col"))
    return jax.shard_map(body, mesh=mesh, in_specs=in_specs, out_specs=out_specs, check_vma=False)
```

```python
import functools

import jax
import jax.numpy as jnp
from jax import lax
from jax.experimental import pallas as pl
from jax.experimental.pallas import tpu as pltpu
from jax.sharding import PartitionSpec as P

MESH = pl.DeviceIdType.MESH
F32 = jnp.float32
FAR = (2, 1, 3)
FAR_Z = (4, 3, 5, 2, 6, 1, 7)
BF16 = jnp.bfloat16

FEAT = 64
PROBES = 32
NX, NY, NZ = 4, 4, 8
TILE = 1024
ITEM = 512
HALF = 16

STEPS = (
    ((0, 0), (1, 0), 1),
    ((0, 1), (0, 3), 0),
    ((0, 1), (0, 3), 1),
    ((1, 1), (1, 3), 0),
    ((1, 1), (1, 3), 1),
    ((0, 2), (1, 2), 1),
    ((0, 2), (1, 2), 0),
    ((0, 0), (1, 0), 0),
)
PASS_ON = {1: 1, 3: 3, 4: 6}
ADD_UP = {3: 1, 5: 3, 6: 6}


def look(values, at):
    out = jnp.int32(values[0])
    for k, v in enumerate(values[1:], 1):
        out = jnp.where(at == k, jnp.int32(v), out)
    return out


def parts3(v):
    hi = v.astype(BF16).astype(F32)
    mid = (v - hi).astype(BF16).astype(F32)
    return hi, mid, v - hi - mid


def kernel(
    row_scale, col_scale,
    rf_hbm, ra_hbm, rs_hbm, cf_hbm, ca_hbm, cw_hbm, cp_hbm,
    out_rows, back_in,
    rf_ref, ra_ref, rs_ref, cf_ref, ca_ref, cw_ref, cp_ref, in_s,
    zbuf, rows, send_cols, recv_cols, relay, cx, cr, xct, small, acc_col,
    keep, core_out, core_in, axis_out, axis_in,
    mid_out, mid_in, z_out, z_in, back_out, back_relay,
    col_s, col_r, z_s, z_r, m_s, m_r, g_s, g_r, f_s,
    core_s, core_r, axis_s, axis_r, mm_s, mm_r, zz_s, zz_r, back_s, back_r,
):
    row = lax.axis_index("row")
    col = lax.axis_index("col")
    y, core = row % 4, col % 2
    x, z = col // 8, (row // 4) * 4 + (col // 2) % 4

    def at(px, py, pz, pc):
        return {"row": (pz // 4) * 4 + py, "col": (px * 4 + pz % 4) * 2 + pc}

    def z_peer(d):
        return at(x, y, (z + d) % NZ, core)

    def axis_peer(t, d):
        return at((x + jnp.where(t == 0, d, 0)) % NX, (y + jnp.where(t == 1, d, 0)) % NY, z, core)

    sibling = at(x, y, z, 1 - core)
    far = (row + 4) % 8

    def row_of(d, other):
        return ((row // 4 + other) % 2) * 4 + (y + d) % 4

    def exchange(out, into, through, send, recv):
        def over_z(d):
            return pltpu.make_async_remote_copy(
                src_ref=out.at[row_of(d, 1)], dst_ref=through.at[d] if d else into.at[row],
                send_sem=send.at[0, d], recv_sem=recv.at[0, d], device_id=z_peer(4), device_id_type=MESH)

        def over_y(d):
            return pltpu.make_async_remote_copy(
                src_ref=out.at[row_of(d, 0)], dst_ref=into.at[row],
                send_sem=send.at[1, d], recv_sem=recv.at[1, d], device_id=axis_peer(1, d), device_id_type=MESH)

        def onward(d):
            return pltpu.make_async_remote_copy(
                src_ref=through.at[d], dst_ref=into.at[far],
                send_sem=send.at[2, d], recv_sem=recv.at[2, d], device_id=axis_peer(1, d), device_id_type=MESH)

        first = [over_z(d) for d in (2, 1, 3, 0)]
        second = [over_y(d) for d in (2, 1, 3)]
        third = [onward(d) for d in (2, 1, 3)]

        def start():
            for c in first + second:
                c.start()
            into[row] = out[row]

        def forward(begin, end):
            for a, b in zip(first[begin:end], third[begin:end]):
                a.wait_recv()
                b.start()

        def finish():
            for c in second + [first[3]] + third:
                c.wait_recv()

        def sent():
            for c in first + second + third:
                c.wait_send()

        return start, forward, finish, sent

    loads = [
        pltpu.make_async_copy(src, dst, in_s.at[k])
        for k, (src, dst) in enumerate((
            (rf_hbm, rf_ref), (ra_hbm, ra_ref), (rs_hbm, rs_ref), (cf_hbm, cf_ref),
            (cp_hbm, cp_ref), (ca_hbm, ca_ref), (cw_hbm, cw_ref)))
    ]
    for c in loads:
        c.start()

    barrier = pltpu.get_barrier_semaphore()
    peers = [z_peer(d) for d in range(1, NZ)] + [sibling]
    peers += [axis_peer(t, d) for t in range(2) for d in range(1, 4)]
    for peer in peers:
        pl.semaphore_signal(barrier, inc=1, device_id=peer, device_id_type=MESH)

    for c in loads[:3]:
        c.wait()
    n = 2 * HALF
    rf = rf_ref[...].astype(F32)
    sq = -0.5 * jnp.sum(rf * rf, axis=1, keepdims=True)
    at8 = lax.broadcasted_iota(jnp.int32, (8, n), 0)
    side = jnp.concatenate(
        [jnp.zeros((64, n), F32), jnp.where(at8 == 6, ra_ref[...].astype(F32), 0.0),
         rs_ref[...].astype(F32), jnp.zeros((24, n), F32)], axis=0)
    side = jnp.concatenate([side, jnp.zeros((128, 128 - n), F32)], axis=1).T[:n]
    lane = lax.broadcasted_iota(jnp.int32, (n, 128), 1)
    mine = side + jnp.concatenate([rf, jnp.zeros((n, 64), F32)], axis=1)
    mine = jnp.where(jnp.logical_and(lane >= 64, lane < 67), 1.0, mine)
    for k, v in enumerate(parts3(sq)):
        mine = jnp.where(lane == 67 + k, v, mine)
    zbuf[z] = mine.astype(BF16)

    for c in loads[3:5]:
        c.wait()
    for p in range(8):
        span = slice(p * TILE, (p + 1) * TILE)
        feats = cf_ref[:, span].astype(F32)
        probes = cp_ref[:, span].astype(F32)
        left = jnp.concatenate([feats[:, :512], feats[:, 512:]], axis=0)
        right = jnp.concatenate([probes[:, q * 256:(q + 1) * 256] for q in range(4)], axis=0)
        send_cols[p] = jnp.concatenate([left, right], axis=1).astype(BF16)

    for c in loads[5:]:
        c.wait()
    eight = pl.ds(pl.multiple_of(row * 8, 8), 8)
    weight = cw_ref[eight, :]
    small[...] = ca_ref[...].astype(F32)
    alpha = small[eight, :]
    weight = jnp.concatenate([weight[k:k + 1] for k in range(8)], axis=1) * (-0.5 / PROBES)
    alpha = jnp.concatenate([alpha[k:k + 1] for k in range(8)], axis=1) * 0.5
    xct[:, 128:] = jnp.ones((TILE, 128), BF16)
    acc_col[...] = jnp.zeros_like(acc_col)

    pl.semaphore_wait(barrier, len(peers))

    def z_copy(d):
        return pltpu.make_async_remote_copy(
            src_ref=zbuf.at[z], dst_ref=zbuf.at[z],
            send_sem=z_s.at[d], recv_sem=z_r.at[d], device_id=z_peer(d), device_id_type=MESH)

    own = (x * 2 + core, y * 2 + core)
    place = (y, x)

    def m_copy(t, d):
        return pltpu.make_async_remote_copy(
            src_ref=rows.at[t, own[t], place[t]], dst_ref=rows.at[t, own[t], place[t]],
            send_sem=m_s.at[t, d], recv_sem=m_r.at[t, d], device_id=axis_peer(1 - t, d), device_id_type=MESH)

    def g_copy(t, g, peer, send_sem):
        return pltpu.make_async_remote_copy(
            src_ref=rows.at[t, g], dst_ref=rows.at[t, g],
            send_sem=send_sem, recv_sem=g_r.at[t, g], device_id=peer, device_id_type=MESH)

    def group(t, d, dc):
        return jnp.where(t == 0, (x + d) % NX, (y + d) % NY) * 2 + (core + dc) % 2

    def axis_copy(t, d):
        return g_copy(t, group(t, 0, 0), axis_peer(t, d), g_s.at[t, d])

    def sibling_copy(t, d):
        return g_copy(t, group(t, d, 0), sibling, f_s.at[t, d])

    z_copies = [z_copy(d) for d in FAR_Z]
    for c in z_copies:
        c.start()
    col_start, col_forward, col_finish, col_sent = exchange(send_cols, recv_cols, relay, col_s, col_r)
    col_start()
    for c in z_copies:
        c.wait_recv()
    m_copies = []
    for t in range(2):
        rows[t, own[t], place[t]] = zbuf[:, t * HALF:(t + 1) * HALF]
        m_copies.append([m_copy(t, d) for d in FAR])
        for c in m_copies[t]:
            c.start()
    col_forward(0, 3)
    for t in range(2):
        for c in m_copies[t]:
            c.wait_recv()
        sibling_copy(t, 0).start()
    for d in (1, 3):
        axis_copy(0, d).start()
    for d in (1, 3):
        axis_copy(1, d).start()
    col_finish()

    feats = jnp.concatenate(
        [jnp.concatenate([recv_cols[p, :, 0:512].astype(F32)[8 * k:8 * k + 8] for k in range(2)], axis=1)
         for p in range(8)], axis=0)
    probes = []
    for p in range(8):
        block = recv_cols[p, :, 512:768].astype(F32)
        probes.append(jnp.concatenate([block[4 * q:4 * q + 4] for q in range(4)], axis=1))
    probes = jnp.concatenate(probes, axis=0)
    sq = parts3(-0.5 * jnp.sum(feats * feats, axis=0, keepdims=True))
    at8 = lax.broadcasted_iota(jnp.int32, (8, TILE), 0)
    side = jnp.where(at8 < 6, 1.0, 0.0)
    for k, v in enumerate(sq):
        side = jnp.where(at8 == k, v, side)
    cx[...] = jnp.concatenate([feats, side, jnp.zeros((56, TILE), F32)], axis=0).astype(BF16)
    cr[...] = jnp.concatenate(
        [jnp.zeros((64, TILE), F32), jnp.where(at8 == 6, alpha, 0.0), weight * probes,
         jnp.zeros((24, TILE), F32)], axis=0).astype(BF16)
    xct[:, 0:128] = jnp.concatenate([feats, feats], axis=0).T.astype(BF16)

    low = lax.broadcasted_iota(jnp.int32, (ITEM, 128), 1) < 64

    def products(r):
        cross = jnp.dot(r, cx[...], preferred_element_type=F32)
        weights = jnp.dot(r, cr[...], preferred_element_type=F32)
        prod = (weights * jnp.exp(cross)).astype(BF16)
        out = jnp.dot(prod, xct[...], preferred_element_type=F32)
        acc_col[...] += jnp.dot(r.T[0:80], prod, preferred_element_type=F32)
        return out

    def pack(out, r):
        def pick(v, k):
            return v.reshape(2 * ITEM // HALF, 2, 8, 128)[:, k].reshape(ITEM, 128)

        wide = r.astype(F32)
        feats = jnp.where(low, pick(wide, 0), pltpu.roll(pick(wide, 1), 64, axis=1))
        toward, total = out[:, :128], out[:, 128:]
        return (jnp.where(low, pick(toward, 0), pick(toward, 1))
                - jnp.where(low, pick(total, 0), pick(total, 1)) * feats)

    def core_copy(t, d):
        return pltpu.make_async_remote_copy(
            src_ref=core_out.at[t, d], dst_ref=core_in.at[t, d],
            send_sem=core_s.at[t, d], recv_sem=core_r.at[t, d], device_id=sibling, device_id_type=MESH)

    def part_copy(t, d):
        return pltpu.make_async_remote_copy(
            src_ref=axis_out.at[t, d], dst_ref=axis_in.at[t, d],
            send_sem=axis_s.at[t, d], recv_sem=axis_r.at[t, d], device_id=axis_peer(t, d), device_id_type=MESH)

    def pairs(s):
        return [[look([o[k][i] for o in STEPS], s) for i in range(2)] for k in range(2)]

    def some(table, s):
        return look([table.get(k, -1) for k in range(len(STEPS))], s)

    def begin(s, two, dc):
        passed = some(PASS_ON, s)

        @pl.when(passed >= 0)
        def _():
            for t, d in pairs(passed):
                g_copy(t, group(t, d, 0), sibling, f_s.at[t, 0]).wait_recv()
                sibling_copy(t, d).start()

        @pl.when(dc == 1)
        def _():
            for t, d in two:
                g_copy(t, group(t, d, 1), sibling, f_s.at[t, 0]).wait_recv()

    def end(packed, s, two, dc):
        half = ITEM // 2
        added = some(ADD_UP, s)

        @pl.when(dc == 0)
        def _():
            for k, (t, d) in enumerate(two):
                keep[t, d] = packed[k * half:(k + 1) * half]

        @pl.when(dc == 1)
        def _():
            for k, (t, d) in enumerate(two):
                core_out[t, d] = packed[k * half:(k + 1) * half].astype(BF16)
                core_copy(t, d).start()

        @pl.when(added >= 0)
        def _():
            for t, d in pairs(added):
                core_copy(t, d).wait_recv()
                axis_out[t, d] = (keep[t, d] + core_in[t, d].astype(F32)).astype(BF16)
                part_copy(t, d).start()

    def step(s, _):
        two, dc = pairs(s), look([o[2] for o in STEPS], s)

        @pl.when(s == 1)
        def _():
            for t in range(2):
                axis_copy(t, 2).start()

        begin(s, two, dc)
        r = jnp.concatenate([rows[t, group(t, d, dc)].reshape(ITEM, 128) for t, d in two], axis=0)
        end(pack(products(r), r), s, two, dc)
        return 0

    lax.fori_loop(0, len(STEPS), step, 0)

    grad = (acc_col[0:64] - acc_col[64:65] * cx[0:64].astype(F32)) * col_scale
    for p in range(8):
        block = grad[8 * p:8 * p + 8]
        back_out[p] = jnp.concatenate([block[:, :512], block[:, 512:]], axis=0).astype(BF16)
    back_start, back_forward, back_finish, back_sent = exchange(back_out, back_in, back_relay, back_s, back_r)
    back_start()

    def mm_copy(t, d):
        return pltpu.make_async_remote_copy(
            src_ref=mid_out.at[t, (place[t] + d) % 4], dst_ref=mid_in.at[t, d],
            send_sem=mm_s.at[t, d], recv_sem=mm_r.at[t, d], device_id=axis_peer(1 - t, d), device_id_type=MESH)

    mm_copies = []
    for t in range(2):
        core_copy(t, 0).wait_recv()
        total = keep[t, 0] + core_in[t, 0].astype(F32)
        for d in range(1, 4):
            part_copy(t, d).wait_recv()
            total += axis_in[t, d].astype(F32)
        keep[t, 0] = total
        mid_out[t] = total.reshape(4, 64, 128).astype(BF16)
        mm_copies.append([mm_copy(t, d) for d in FAR])
        for c in mm_copies[t]:
            c.start()

    blocks = []
    for t in range(2):
        total = keep[t, 0, pl.ds(pl.multiple_of(place[t] * 64, 64), 64), :]
        for c, d in zip(mm_copies[t], FAR):
            c.wait_recv()
            total += mid_in[t, d].astype(F32)
        blocks.append(total.reshape(NZ, 8, 128))
    z_out[...] = jnp.concatenate(blocks, axis=1).astype(BF16)

    def zz_copy(d):
        return pltpu.make_async_remote_copy(
            src_ref=z_out.at[(z + d) % NZ], dst_ref=z_in.at[d],
            send_sem=zz_s.at[d], recv_sem=zz_r.at[d], device_id=z_peer(d), device_id_type=MESH)

    zz_copies = [zz_copy(d) for d in FAR_Z]
    for c in zz_copies:
        c.start()
    back_forward(0, 3)
    total = z_out[z].astype(F32)
    for c, d in zip(zz_copies, FAR_Z):
        c.wait_recv()
        total += z_in[d].astype(F32)
    out_rows[...] = total * row_scale
    back_finish()

    col_sent()
    back_sent()
    for c in z_copies + m_copies[0] + m_copies[1] + mm_copies[0] + mm_copies[1] + zz_copies:
        c.wait_send()
    for t in range(2):
        for d in range(4):
            sibling_copy(t, d).wait_send()
            core_copy(t, d).wait_send()
            if d:
                axis_copy(t, d).wait_send()
                part_copy(t, d).wait_send()


def unpack(rows_ref, cols_ref, out_rows, out_cols):
    total = rows_ref[...]
    moved = pltpu.roll(total, 64, axis=1)
    final = jnp.concatenate([total[0:8], moved[0:8], total[8:16], moved[8:16]], axis=0)
    out_rows[...] = final[:, 0:64]
    for p in range(8):
        block = cols_ref[p].astype(F32)
        out_cols[:, p * TILE:p * TILE + 512] = block[0:8]
        out_cols[:, p * TILE + 512:(p + 1) * TILE] = block[8:16]


def body(row_feats, row_alpha, row_solves, col_feats, col_alpha, col_weight, col_probes):
    row_size = lax.axis_size("row")
    col_size = lax.axis_size("col")
    own_rows = row_alpha.shape[0]
    own_cols = col_alpha.shape[0]
    window = own_rows * row_size * col_size
    points = own_cols * col_size
    dma = pltpu.SemaphoreType.DMA
    vmem = pl.BlockSpec(memory_space=pltpu.VMEM)
    hbm = pl.BlockSpec(memory_space=pltpu.HBM)
    args = (
        row_feats.T, row_alpha.reshape(1, -1), row_solves, col_feats,
        col_alpha.reshape(-1, 128), col_weight.reshape(-1, 128), col_probes,
    )
    half = ITEM // 2
    totals = pl.pallas_call(
        functools.partial(kernel, 1.0 / points**0.5, 1.0 / window**0.5),
        out_shape=(
            jax.ShapeDtypeStruct((16, 128), F32),
            jax.ShapeDtypeStruct((8, 16, 512), BF16),
        ),
        in_specs=[hbm] * 7,
        out_specs=(vmem, vmem),
        scratch_shapes=[
            *[pltpu.VMEM(a.shape, a.dtype) for a in args],
            dma((7,)),
            pltpu.VMEM((NZ, 2 * HALF, 128), BF16),
            pltpu.VMEM((2, 8, 4, NZ, HALF, 128), BF16),
            pltpu.VMEM((8, 16, 768), BF16),
            pltpu.VMEM((8, 16, 768), BF16),
            pltpu.VMEM((4, 16, 768), BF16),
            pltpu.VMEM((128, TILE), BF16),
            pltpu.VMEM((128, TILE), BF16),
            pltpu.VMEM((TILE, 256), BF16),
            pltpu.VMEM((own_cols // 128, 128), F32),
            pltpu.VMEM((80, TILE), F32),
            pltpu.VMEM((2, 4, half, 128), F32),
            *[pltpu.VMEM((2, 4, half, 128), BF16)] * 4,
            *[pltpu.VMEM((2, 4, half // 4, 128), BF16)] * 2,
            *[pltpu.VMEM((NZ, 16, 128), BF16)] * 2,
            pltpu.VMEM((8, 16, 512), BF16),
            pltpu.VMEM((4, 16, 512), BF16),
            dma((3, 4)), dma((3, 4)), dma((NZ,)), dma((NZ,)), dma((2, 4)), dma((2, 4)),
            dma((2, 4)), dma((2, 8)), dma((2, 4)),
            *[dma((2, 4))] * 6,
            dma((NZ,)), dma((NZ,)), dma((3, 4)), dma((3, 4)),
        ],
        compiler_params=pltpu.CompilerParams(
            collective_id=0, has_side_effects=True, vmem_limit_bytes=63 * 2**20),
        name="evidence_gradients",
    )(*args)
    grad_rows, grad_cols = pl.pallas_call(
        unpack,
        out_shape=(
            jax.ShapeDtypeStruct((own_rows, FEAT), F32),
            jax.ShapeDtypeStruct((FEAT // row_size, own_cols), F32),
        ),
        in_specs=[vmem] * 2,
        out_specs=(vmem, vmem),
        name="unpack_gradients",
    )(*totals)
    return grad_rows.T, grad_cols


def solution(mesh):
    in_specs = (
        P(None, ("row", "col")),
        P(("row", "col")),
        P(None, ("row", "col")),
        P("row", "col"),
        P("col"),
        P("col"),
        P("row", "col"),
    )
    out_specs = (P(None, ("row", "col")), P("row", "col"))
    return jax.shard_map(body, mesh=mesh, in_specs=in_specs, out_specs=out_specs, check_vma=False)
```

```python
import functools

import jax
import jax.numpy as jnp
from jax import lax
from jax.experimental import pallas as pl
from jax.experimental.pallas import tpu as pltpu
from jax.sharding import PartitionSpec as P

MESH = pl.DeviceIdType.MESH
F32 = jnp.float32
FAR = (2, 1, 3)
FAR_Z = (4, 3, 5, 2, 6, 1, 7)
BF16 = jnp.bfloat16

FEAT = 64
PROBES = 32
NX, NY, NZ = 4, 4, 8
TILE = 1024
ITEM = 512
HALF = 16

STEPS = (
    ((0, 0), (1, 0), 1),
    ((0, 1), (0, 3), 0),
    ((0, 1), (0, 3), 1),
    ((1, 1), (1, 3), 0),
    ((1, 1), (1, 3), 1),
    ((0, 2), (1, 2), 1),
    ((0, 2), (1, 2), 0),
    ((0, 0), (1, 0), 0),
)
PASS_ON = {1: 1, 3: 3, 4: 6}
ADD_UP = {3: 1, 5: 3, 6: 6}


def look(values, at):
    out = jnp.int32(values[0])
    for k, v in enumerate(values[1:], 1):
        out = jnp.where(at == k, jnp.int32(v), out)
    return out


def parts3(v):
    hi = v.astype(BF16).astype(F32)
    mid = (v - hi).astype(BF16).astype(F32)
    return hi, mid, v - hi - mid


def kernel(
    col_scale,
    rf_hbm, ra_hbm, rs_hbm, cf_hbm, ca_hbm, cw_hbm, cp_hbm,
    z_in, back_in,
    rf_ref, ra_ref, rs_ref, cf_ref, ca_ref, cw_ref, cp_ref, in_s,
    zbuf, rows, send_cols, recv_cols, relay, cx, cr, xct, small, acc_col,
    keep, core_out, core_in, axis_out, axis_in,
    mid_out, mid_in, z_out, back_out, back_relay,
    col_s, col_r, z_s, z_r, m_s, m_r, g_s, g_r, f_s,
    core_s, core_r, axis_s, axis_r, mm_s, mm_r, zz_s, zz_r, back_s, back_r,
):
    row = lax.axis_index("row")
    col = lax.axis_index("col")
    y, core = row % 4, col % 2
    x, z = col // 8, (row // 4) * 4 + (col // 2) % 4

    def at(px, py, pz, pc):
        return {"row": (pz // 4) * 4 + py, "col": (px * 4 + pz % 4) * 2 + pc}

    def z_peer(d):
        return at(x, y, (z + d) % NZ, core)

    def axis_peer(t, d):
        return at((x + jnp.where(t == 0, d, 0)) % NX, (y + jnp.where(t == 1, d, 0)) % NY, z, core)

    sibling = at(x, y, z, 1 - core)
    far = (row + 4) % 8

    def row_of(d, other):
        return ((row // 4 + other) % 2) * 4 + (y + d) % 4

    def exchange(out, into, through, send, recv):
        def over_z(d):
            return pltpu.make_async_remote_copy(
                src_ref=out.at[row_of(d, 1)], dst_ref=through.at[d] if d else into.at[row],
                send_sem=send.at[0, d], recv_sem=recv.at[0, d], device_id=z_peer(4), device_id_type=MESH)

        def over_y(d):
            return pltpu.make_async_remote_copy(
                src_ref=out.at[row_of(d, 0)], dst_ref=into.at[row],
                send_sem=send.at[1, d], recv_sem=recv.at[1, d], device_id=axis_peer(1, d), device_id_type=MESH)

        def onward(d):
            return pltpu.make_async_remote_copy(
                src_ref=through.at[d], dst_ref=into.at[far],
                send_sem=send.at[2, d], recv_sem=recv.at[2, d], device_id=axis_peer(1, d), device_id_type=MESH)

        first = [over_z(d) for d in (2, 1, 3, 0)]
        second = [over_y(d) for d in (2, 1, 3)]
        third = [onward(d) for d in (2, 1, 3)]

        mine = pltpu.make_async_copy(out.at[row], into.at[row], send.at[1, 0])

        def start():
            for c in first + second:
                c.start()
            mine.start()

        def forward(begin, end):
            for a, b in zip(first[begin:end], third[begin:end]):
                a.wait_recv()
                b.start()

        def finish():
            for c in second + [first[3]] + third:
                c.wait_recv()
            mine.wait()

        def sent():
            for c in first + second + third:
                c.wait_send()

        return start, forward, finish, sent

    loads = [
        pltpu.make_async_copy(src, dst, in_s.at[k])
        for k, (src, dst) in enumerate((
            (rf_hbm, rf_ref), (ra_hbm, ra_ref), (rs_hbm, rs_ref), (cf_hbm, cf_ref),
            (cp_hbm, cp_ref), (ca_hbm, ca_ref), (cw_hbm, cw_ref)))
    ]
    barrier = pltpu.get_barrier_semaphore()
    peers = [z_peer(d) for d in FAR_Z]
    peers += [axis_peer(t, d) for t in range(2) for d in FAR] + [sibling]
    for peer in peers:
        pl.semaphore_signal(barrier, inc=1, device_id=peer, device_id_type=MESH)
    for c in loads:
        c.start()

    for c in loads[:3]:
        c.wait()
    n = 2 * HALF
    rf = rf_ref[...].astype(F32)
    sq = -0.5 * jnp.sum(rf * rf, axis=1, keepdims=True)
    at8 = lax.broadcasted_iota(jnp.int32, (8, n), 0)
    side = jnp.concatenate(
        [jnp.zeros((64, n), F32), jnp.where(at8 == 6, ra_ref[...].astype(F32), 0.0),
         rs_ref[...].astype(F32), jnp.zeros((24, n), F32)], axis=0)
    side = jnp.concatenate([side, jnp.zeros((128, 128 - n), F32)], axis=1).T[:n]
    lane = lax.broadcasted_iota(jnp.int32, (n, 128), 1)
    mine = side + jnp.concatenate([rf, jnp.zeros((n, 64), F32)], axis=1)
    mine = jnp.where(jnp.logical_and(lane >= 64, lane < 67), 1.0, mine)
    for k, v in enumerate(parts3(sq)):
        mine = jnp.where(lane == 67 + k, v, mine)
    zbuf[z] = mine.astype(BF16)

    for c in loads[3:5]:
        c.wait()
    for p in range(8):
        span = slice(p * TILE, (p + 1) * TILE)
        feats = cf_ref[:, span].astype(F32)
        probes = cp_ref[:, span].astype(F32)
        left = jnp.concatenate([feats[:, :512], feats[:, 512:]], axis=0)
        right = jnp.concatenate([probes[:, q * 256:(q + 1) * 256] for q in range(4)], axis=0)
        send_cols[p] = jnp.concatenate([left, right], axis=1).astype(BF16)

    for c in loads[5:]:
        c.wait()
    eight = pl.ds(pl.multiple_of(row * 8, 8), 8)
    weight = cw_ref[eight, :]
    small[...] = ca_ref[...].astype(F32)
    alpha = small[eight, :]
    weight = jnp.concatenate([weight[k:k + 1] for k in range(8)], axis=1) * (-0.5 / PROBES)
    alpha = jnp.concatenate([alpha[k:k + 1] for k in range(8)], axis=1) * 0.5
    xct[:, 128:] = jnp.ones((TILE, 128), BF16)
    acc_col[...] = jnp.zeros_like(acc_col)

    pl.semaphore_wait(barrier, len(peers))

    def z_copy(d):
        return pltpu.make_async_remote_copy(
            src_ref=zbuf.at[z], dst_ref=zbuf.at[z],
            send_sem=z_s.at[d], recv_sem=z_r.at[d], device_id=z_peer(d), device_id_type=MESH)

    own = (x * 2 + core, y * 2 + core)
    place = (y, x)

    def m_copy(t, d):
        return pltpu.make_async_remote_copy(
            src_ref=rows.at[t, own[t], place[t]], dst_ref=rows.at[t, own[t], place[t]],
            send_sem=m_s.at[t, d], recv_sem=m_r.at[t, d], device_id=axis_peer(1 - t, d), device_id_type=MESH)

    def g_copy(t, g, peer, send_sem):
        return pltpu.make_async_remote_copy(
            src_ref=rows.at[t, g], dst_ref=rows.at[t, g],
            send_sem=send_sem, recv_sem=g_r.at[t, g], device_id=peer, device_id_type=MESH)

    def group(t, d, dc):
        return jnp.where(t == 0, (x + d) % NX, (y + d) % NY) * 2 + (core + dc) % 2

    def axis_copy(t, d):
        return g_copy(t, group(t, 0, 0), axis_peer(t, d), g_s.at[t, d])

    def sibling_copy(t, d):
        return g_copy(t, group(t, d, 0), sibling, f_s.at[t, d])

    z_copies = [z_copy(d) for d in FAR_Z]
    for c in z_copies:
        c.start()
    col_start, col_forward, col_finish, col_sent = exchange(send_cols, recv_cols, relay, col_s, col_r)
    col_start()
    for c in z_copies:
        c.wait_recv()
    m_copies = []
    for t in range(2):
        rows[t, own[t], place[t]] = zbuf[:, t * HALF:(t + 1) * HALF]
        m_copies.append([m_copy(t, d) for d in FAR])
        for c in m_copies[t]:
            c.start()
    col_forward(0, 3)
    for t in range(2):
        for c in m_copies[t]:
            c.wait_recv()
        sibling_copy(t, 0).start()
    for d in (1, 3):
        axis_copy(0, d).start()
    for d in (1, 3):
        axis_copy(1, d).start()
    col_finish()

    feats = jnp.concatenate(
        [jnp.concatenate([recv_cols[p, :, 0:512].astype(F32)[8 * k:8 * k + 8] for k in range(2)], axis=1)
         for p in range(8)], axis=0)
    probes = []
    for p in range(8):
        block = recv_cols[p, :, 512:768].astype(F32)
        probes.append(jnp.concatenate([block[4 * q:4 * q + 4] for q in range(4)], axis=1))
    probes = jnp.concatenate(probes, axis=0)
    sq = parts3(-0.5 * jnp.sum(feats * feats, axis=0, keepdims=True))
    at8 = lax.broadcasted_iota(jnp.int32, (8, TILE), 0)
    side = jnp.where(at8 < 6, 1.0, 0.0)
    for k, v in enumerate(sq):
        side = jnp.where(at8 == k, v, side)
    cx[...] = jnp.concatenate([feats, side, jnp.zeros((56, TILE), F32)], axis=0).astype(BF16)
    cr[...] = jnp.concatenate(
        [jnp.zeros((64, TILE), F32), jnp.where(at8 == 6, alpha, 0.0), weight * probes,
         jnp.zeros((24, TILE), F32)], axis=0).astype(BF16)
    xct[:, 0:128] = jnp.concatenate([feats, feats], axis=0).T.astype(BF16)

    low = lax.broadcasted_iota(jnp.int32, (ITEM, 128), 1) < 64

    def products(r):
        cross = jnp.dot(r, cx[...], preferred_element_type=F32)
        weights = jnp.dot(r, cr[...], preferred_element_type=F32)
        prod = (weights * jnp.exp(cross)).astype(BF16)
        out = jnp.dot(prod, xct[...], preferred_element_type=F32)
        acc_col[...] += jnp.dot(r.T[0:80], prod, preferred_element_type=F32)
        return out

    def pack(out, r):
        def pick(v, k):
            return v.reshape(2 * ITEM // HALF, 2, 8, 128)[:, k].reshape(ITEM, 128)

        wide = r.astype(F32)
        feats = jnp.where(low, pick(wide, 0), pltpu.roll(pick(wide, 1), 64, axis=1))
        toward, total = out[:, :128], out[:, 128:]
        return (jnp.where(low, pick(toward, 0), pick(toward, 1))
                - jnp.where(low, pick(total, 0), pick(total, 1)) * feats)

    def core_copy(t, d):
        return pltpu.make_async_remote_copy(
            src_ref=core_out.at[t, d], dst_ref=core_in.at[t, d],
            send_sem=core_s.at[t, d], recv_sem=core_r.at[t, d], device_id=sibling, device_id_type=MESH)

    def part_copy(t, d):
        return pltpu.make_async_remote_copy(
            src_ref=axis_out.at[t, d], dst_ref=axis_in.at[t, d],
            send_sem=axis_s.at[t, d], recv_sem=axis_r.at[t, d], device_id=axis_peer(t, d), device_id_type=MESH)

    def pairs(s):
        return [[look([o[k][i] for o in STEPS], s) for i in range(2)] for k in range(2)]

    def some(table, s):
        return look([table.get(k, -1) for k in range(len(STEPS))], s)

    def begin(s, two, dc):
        passed = some(PASS_ON, s)

        @pl.when(passed >= 0)
        def _():
            for t, d in pairs(passed):
                g_copy(t, group(t, d, 0), sibling, f_s.at[t, 0]).wait_recv()
                sibling_copy(t, d).start()

        @pl.when(dc == 1)
        def _():
            for t, d in two:
                g_copy(t, group(t, d, 1), sibling, f_s.at[t, 0]).wait_recv()

    def end(packed, s, two, dc):
        half = ITEM // 2
        added = some(ADD_UP, s)

        @pl.when(dc == 0)
        def _():
            for k, (t, d) in enumerate(two):
                keep[t, d] = packed[k * half:(k + 1) * half]

        @pl.when(dc == 1)
        def _():
            for k, (t, d) in enumerate(two):
                core_out[t, d] = packed[k * half:(k + 1) * half].astype(BF16)
                core_copy(t, d).start()

        @pl.when(added >= 0)
        def _():
            for t, d in pairs(added):
                core_copy(t, d).wait_recv()
                axis_out[t, d] = (keep[t, d] + core_in[t, d].astype(F32)).astype(BF16)
                part_copy(t, d).start()

    def step(s, _):
        two, dc = pairs(s), look([o[2] for o in STEPS], s)

        @pl.when(s == 1)
        def _():
            for t in range(2):
                axis_copy(t, 2).start()

        begin(s, two, dc)
        r = jnp.concatenate([rows[t, group(t, d, dc)].reshape(ITEM, 128) for t, d in two], axis=0)
        end(pack(products(r), r), s, two, dc)
        return 0

    lax.fori_loop(0, len(STEPS), step, 0)

    grad = (acc_col[0:64] - acc_col[64:65] * cx[0:64].astype(F32)) * col_scale
    for p in range(8):
        block = grad[8 * p:8 * p + 8]
        back_out[p] = jnp.concatenate([block[:, :512], block[:, 512:]], axis=0).astype(BF16)
    back_start, back_forward, back_finish, back_sent = exchange(back_out, back_in, back_relay, back_s, back_r)
    back_start()

    def mm_copy(t, d):
        return pltpu.make_async_remote_copy(
            src_ref=mid_out.at[t, (place[t] + d) % 4], dst_ref=mid_in.at[t, d],
            send_sem=mm_s.at[t, d], recv_sem=mm_r.at[t, d], device_id=axis_peer(1 - t, d), device_id_type=MESH)

    mm_copies = []
    for t in range(2):
        core_copy(t, 0).wait_recv()
        total = keep[t, 0] + core_in[t, 0].astype(F32)
        for d in range(1, 4):
            part_copy(t, d).wait_recv()
            total += axis_in[t, d].astype(F32)
        keep[t, 0] = total
        mid_out[t] = total.reshape(4, 64, 128).astype(BF16)
        mm_copies.append([mm_copy(t, d) for d in FAR])
        for c in mm_copies[t]:
            c.start()

    blocks = []
    for t in range(2):
        total = keep[t, 0, pl.ds(pl.multiple_of(place[t] * 64, 64), 64), :]
        for c, d in zip(mm_copies[t], FAR):
            c.wait_recv()
            total += mid_in[t, d].astype(F32)
        blocks.append(total.reshape(NZ, 8, 128))
    z_out[...] = jnp.concatenate(blocks, axis=1).astype(BF16)

    def zz_copy(d):
        return pltpu.make_async_remote_copy(
            src_ref=z_out.at[(z + d) % NZ], dst_ref=z_in.at[d],
            send_sem=zz_s.at[d], recv_sem=zz_r.at[d], device_id=z_peer(d), device_id_type=MESH)

    zz_copies = [zz_copy(d) for d in FAR_Z]
    for c in zz_copies:
        c.start()
    mine = pltpu.make_async_copy(z_out.at[z], z_in.at[0], zz_s.at[0])
    mine.start()
    back_forward(0, 3)
    for c in zz_copies:
        c.wait_recv()
    mine.wait()
    back_finish()

    col_sent()
    back_sent()
    for c in z_copies + m_copies[0] + m_copies[1] + mm_copies[0] + mm_copies[1] + zz_copies:
        c.wait_send()
    for t in range(2):
        for d in range(4):
            sibling_copy(t, d).wait_send()
            core_copy(t, d).wait_send()
            if d:
                axis_copy(t, d).wait_send()
                part_copy(t, d).wait_send()


def unpack(row_scale, rows_ref, cols_ref, out_rows, out_cols):
    total = rows_ref[0].astype(F32)
    for d in range(1, NZ):
        total += rows_ref[d].astype(F32)
    total = total * row_scale
    moved = pltpu.roll(total, 64, axis=1)
    final = jnp.concatenate([total[0:8], moved[0:8], total[8:16], moved[8:16]], axis=0)
    out_rows[...] = final[:, 0:64]
    for p in range(8):
        block = cols_ref[p].astype(F32)
        out_cols[:, p * TILE:p * TILE + 512] = block[0:8]
        out_cols[:, p * TILE + 512:(p + 1) * TILE] = block[8:16]


def body(row_feats, row_alpha, row_solves, col_feats, col_alpha, col_weight, col_probes):
    row_size = lax.axis_size("row")
    col_size = lax.axis_size("col")
    own_rows = row_alpha.shape[0]
    own_cols = col_alpha.shape[0]
    window = own_rows * row_size * col_size
    points = own_cols * col_size
    dma = pltpu.SemaphoreType.DMA
    vmem = pl.BlockSpec(memory_space=pltpu.VMEM)
    hbm = pl.BlockSpec(memory_space=pltpu.HBM)
    args = (
        row_feats.T, row_alpha.reshape(1, -1), row_solves, col_feats,
        col_alpha.reshape(-1, 128), col_weight.reshape(-1, 128), col_probes,
    )
    half = ITEM // 2
    totals = pl.pallas_call(
        functools.partial(kernel, 1.0 / window**0.5),
        out_shape=(
            jax.ShapeDtypeStruct((NZ, 16, 128), BF16),
            jax.ShapeDtypeStruct((8, 16, 512), BF16),
        ),
        in_specs=[hbm] * 7,
        out_specs=(hbm, hbm),
        scratch_shapes=[
            *[pltpu.VMEM(a.shape, a.dtype) for a in args],
            dma((7,)),
            pltpu.VMEM((NZ, 2 * HALF, 128), BF16),
            pltpu.VMEM((2, 8, 4, NZ, HALF, 128), BF16),
            pltpu.VMEM((8, 16, 768), BF16),
            pltpu.VMEM((8, 16, 768), BF16),
            pltpu.VMEM((4, 16, 768), BF16),
            pltpu.VMEM((128, TILE), BF16),
            pltpu.VMEM((128, TILE), BF16),
            pltpu.VMEM((TILE, 256), BF16),
            pltpu.VMEM((own_cols // 128, 128), F32),
            pltpu.VMEM((80, TILE), F32),
            pltpu.VMEM((2, 4, half, 128), F32),
            *[pltpu.VMEM((2, 4, half, 128), BF16)] * 4,
            *[pltpu.VMEM((2, 4, half // 4, 128), BF16)] * 2,
            pltpu.VMEM((NZ, 16, 128), BF16),
            pltpu.VMEM((8, 16, 512), BF16),
            pltpu.VMEM((4, 16, 512), BF16),
            dma((3, 4)), dma((3, 4)), dma((NZ,)), dma((NZ,)), dma((2, 4)), dma((2, 4)),
            dma((2, 4)), dma((2, 8)), dma((2, 4)),
            *[dma((2, 4))] * 6,
            dma((NZ,)), dma((NZ,)), dma((3, 4)), dma((3, 4)),
        ],
        compiler_params=pltpu.CompilerParams(
            collective_id=0, has_side_effects=True, vmem_limit_bytes=63 * 2**20),
        name="evidence_gradients",
    )(*args)
    grad_rows, grad_cols = pl.pallas_call(
        functools.partial(unpack, 1.0 / points**0.5),
        out_shape=(
            jax.ShapeDtypeStruct((own_rows, FEAT), F32),
            jax.ShapeDtypeStruct((FEAT // row_size, own_cols), F32),
        ),
        in_specs=[vmem] * 2,
        out_specs=(vmem, vmem),
        name="unpack_gradients",
    )(*totals)
    return grad_rows.T, grad_cols


def solution(mesh):
    in_specs = (
        P(None, ("row", "col")),
        P(("row", "col")),
        P(None, ("row", "col")),
        P("row", "col"),
        P("col"),
        P("col"),
        P("row", "col"),
    )
    out_specs = (P(None, ("row", "col")), P("row", "col"))
    return jax.shard_map(body, mesh=mesh, in_specs=in_specs, out_specs=out_specs, check_vma=False)
```

```python
import functools

import jax
import jax.numpy as jnp
from jax import lax
from jax.experimental import pallas as pl
from jax.experimental.pallas import tpu as pltpu
from jax.sharding import PartitionSpec as P

MESH = pl.DeviceIdType.MESH
F32 = jnp.float32
FAR = (2, 1, 3)
FAR_Z = (4, 3, 5, 2, 6, 1, 7)
BF16 = jnp.bfloat16

FEAT = 64
PROBES = 32
NX, NY, NZ = 4, 4, 8
TILE = 1024
ITEM = 512
HALF = 16

STEPS = (
    ((0, 0), (1, 0), 1),
    ((0, 1), (0, 3), 0),
    ((0, 1), (0, 3), 1),
    ((1, 1), (1, 3), 1),
    ((0, 2), (1, 2), 1),
    ((0, 2), (1, 2), 0),
    ((1, 1), (1, 3), 0),
    ((0, 0), (1, 0), 0),
)
PASS_ON = {1: 1, 2: 6, 3: 5}
ADD_UP = {3: 1, 5: 5, 6: 6}


def look(values, at):
    out = jnp.int32(values[0])
    for k, v in enumerate(values[1:], 1):
        out = jnp.where(at == k, jnp.int32(v), out)
    return out


def parts3(v):
    hi = v.astype(BF16).astype(F32)
    mid = (v - hi).astype(BF16).astype(F32)
    return hi, mid, v - hi - mid


def kernel(
    col_scale,
    rf_hbm, ra_hbm, rs_hbm, cf_hbm, ca_hbm, cw_hbm, cp_hbm,
    z_in, back_in,
    rf_ref, ra_ref, rs_ref, cf_ref, ca_ref, cw_ref, cp_ref, in_s,
    zbuf, rows, send_cols, recv_cols, relay, cx, cr, xct, small, acc_col,
    keep, core_out, core_in, axis_out, axis_in,
    mid_out, mid_in, z_out, back_out, back_relay,
    col_s, col_r, z_s, z_r, m_s, m_r, g_s, g_r, f_s,
    core_s, core_r, axis_s, axis_r, mm_s, mm_r, zz_s, zz_r, back_s, back_r,
):
    row = lax.axis_index("row")
    col = lax.axis_index("col")
    y, core = row % 4, col % 2
    x, z = col // 8, (row // 4) * 4 + (col // 2) % 4

    def at(px, py, pz, pc):
        return {"row": (pz // 4) * 4 + py, "col": (px * 4 + pz % 4) * 2 + pc}

    def z_peer(d):
        return at(x, y, (z + d) % NZ, core)

    def axis_peer(t, d):
        return at((x + jnp.where(t == 0, d, 0)) % NX, (y + jnp.where(t == 1, d, 0)) % NY, z, core)

    sibling = at(x, y, z, 1 - core)
    far = (row + 4) % 8

    def row_of(d, other):
        return ((row // 4 + other) % 2) * 4 + (y + d) % 4

    def exchange(out, into, through, send, recv):
        def over_z(d):
            return pltpu.make_async_remote_copy(
                src_ref=out.at[row_of(d, 1)], dst_ref=through.at[d] if d else into.at[row],
                send_sem=send.at[0, d], recv_sem=recv.at[0, d], device_id=z_peer(4), device_id_type=MESH)

        def over_y(d):
            return pltpu.make_async_remote_copy(
                src_ref=out.at[row_of(d, 0)], dst_ref=into.at[row],
                send_sem=send.at[1, d], recv_sem=recv.at[1, d], device_id=axis_peer(1, d), device_id_type=MESH)

        def onward(d):
            return pltpu.make_async_remote_copy(
                src_ref=through.at[d], dst_ref=into.at[far],
                send_sem=send.at[2, d], recv_sem=recv.at[2, d], device_id=axis_peer(1, d), device_id_type=MESH)

        first = [over_z(d) for d in (2, 1, 3, 0)]
        second = [over_y(d) for d in (2, 1, 3)]
        third = [onward(d) for d in (2, 1, 3)]

        mine = pltpu.make_async_copy(out.at[row], into.at[row], send.at[1, 0])

        def start():
            for c in first + second:
                c.start()
            mine.start()

        def forward(begin, end):
            for a, b in zip(first[begin:end], third[begin:end]):
                a.wait_recv()
                b.start()

        def finish():
            for c in second + [first[3]] + third:
                c.wait_recv()
            mine.wait()

        def sent():
            for c in first + second + third:
                c.wait_send()

        return start, forward, finish, sent

    loads = [
        pltpu.make_async_copy(src, dst, in_s.at[k])
        for k, (src, dst) in enumerate((
            (rf_hbm, rf_ref), (ra_hbm, ra_ref), (rs_hbm, rs_ref), (cf_hbm, cf_ref),
            (cp_hbm, cp_ref), (ca_hbm, ca_ref), (cw_hbm, cw_ref)))
    ]
    barrier = pltpu.get_barrier_semaphore()
    peers = [z_peer(d) for d in FAR_Z]
    peers += [axis_peer(t, d) for t in range(2) for d in FAR] + [sibling]
    for peer in peers:
        pl.semaphore_signal(barrier, inc=1, device_id=peer, device_id_type=MESH)
    for c in loads:
        c.start()

    for c in loads[:3]:
        c.wait()
    n = 2 * HALF
    rf = rf_ref[...].astype(F32)
    sq = -0.5 * jnp.sum(rf * rf, axis=1, keepdims=True)
    at8 = lax.broadcasted_iota(jnp.int32, (8, n), 0)
    side = jnp.concatenate(
        [jnp.zeros((64, n), F32), jnp.where(at8 == 6, ra_ref[...].astype(F32), 0.0),
         rs_ref[...].astype(F32), jnp.zeros((24, n), F32)], axis=0)
    side = jnp.concatenate([side, jnp.zeros((128, 128 - n), F32)], axis=1).T[:n]
    lane = lax.broadcasted_iota(jnp.int32, (n, 128), 1)
    mine = side + jnp.concatenate([rf, jnp.zeros((n, 64), F32)], axis=1)
    mine = jnp.where(jnp.logical_and(lane >= 64, lane < 67), 1.0, mine)
    for k, v in enumerate(parts3(sq)):
        mine = jnp.where(lane == 67 + k, v, mine)
    zbuf[z] = mine.astype(BF16)

    for c in loads[3:5]:
        c.wait()
    for p in range(8):
        span = slice(p * TILE, (p + 1) * TILE)
        feats = cf_ref[:, span].astype(F32)
        probes = cp_ref[:, span].astype(F32)
        left = jnp.concatenate([feats[:, :512], feats[:, 512:]], axis=0)
        right = jnp.concatenate([probes[:, q * 256:(q + 1) * 256] for q in range(4)], axis=0)
        send_cols[p] = jnp.concatenate([left, right], axis=1).astype(BF16)

    for c in loads[5:]:
        c.wait()
    eight = pl.ds(pl.multiple_of(row * 8, 8), 8)
    weight = cw_ref[eight, :]
    small[...] = ca_ref[...].astype(F32)
    alpha = small[eight, :]
    weight = jnp.concatenate([weight[k:k + 1] for k in range(8)], axis=1) * (-0.5 / PROBES)
    alpha = jnp.concatenate([alpha[k:k + 1] for k in range(8)], axis=1) * 0.5
    xct[:, 128:] = jnp.ones((TILE, 128), BF16)
    acc_col[...] = jnp.zeros_like(acc_col)

    pl.semaphore_wait(barrier, len(peers))

    def z_copy(d):
        return pltpu.make_async_remote_copy(
            src_ref=zbuf.at[z], dst_ref=zbuf.at[z],
            send_sem=z_s.at[d], recv_sem=z_r.at[d], device_id=z_peer(d), device_id_type=MESH)

    own = (x * 2 + core, y * 2 + core)
    place = (y, x)

    def m_copy(t, d):
        return pltpu.make_async_remote_copy(
            src_ref=rows.at[t, own[t], place[t]], dst_ref=rows.at[t, own[t], place[t]],
            send_sem=m_s.at[t, d], recv_sem=m_r.at[t, d], device_id=axis_peer(1 - t, d), device_id_type=MESH)

    def g_copy(t, g, peer, send_sem):
        return pltpu.make_async_remote_copy(
            src_ref=rows.at[t, g], dst_ref=rows.at[t, g],
            send_sem=send_sem, recv_sem=g_r.at[t, g], device_id=peer, device_id_type=MESH)

    def group(t, d, dc):
        return jnp.where(t == 0, (x + d) % NX, (y + d) % NY) * 2 + (core + dc) % 2

    def axis_copy(t, d):
        return g_copy(t, group(t, 0, 0), axis_peer(t, d), g_s.at[t, d])

    def sibling_copy(t, d):
        return g_copy(t, group(t, d, 0), sibling, f_s.at[t, d])

    z_copies = [z_copy(d) for d in FAR_Z]
    for c in z_copies:
        c.start()
    col_start, col_forward, col_finish, col_sent = exchange(send_cols, recv_cols, relay, col_s, col_r)
    col_start()
    for c in z_copies:
        c.wait_recv()
    m_copies = []
    for t in range(2):
        rows[t, own[t], place[t]] = zbuf[:, t * HALF:(t + 1) * HALF]
        m_copies.append([m_copy(t, d) for d in FAR])
        for c in m_copies[t]:
            c.start()
    col_forward(0, 3)
    for t in range(2):
        for c in m_copies[t]:
            c.wait_recv()
        sibling_copy(t, 0).start()
    for d in (1, 3):
        axis_copy(0, d).start()
    for d in (1, 3):
        axis_copy(1, d).start()
    col_finish()

    feats = jnp.concatenate(
        [jnp.concatenate([recv_cols[p, :, 0:512].astype(F32)[8 * k:8 * k + 8] for k in range(2)], axis=1)
         for p in range(8)], axis=0)
    probes = []
    for p in range(8):
        block = recv_cols[p, :, 512:768].astype(F32)
        probes.append(jnp.concatenate([block[4 * q:4 * q + 4] for q in range(4)], axis=1))
    probes = jnp.concatenate(probes, axis=0)
    sq = parts3(-0.5 * jnp.sum(feats * feats, axis=0, keepdims=True))
    at8 = lax.broadcasted_iota(jnp.int32, (8, TILE), 0)
    side = jnp.where(at8 < 6, 1.0, 0.0)
    for k, v in enumerate(sq):
        side = jnp.where(at8 == k, v, side)
    cx[...] = jnp.concatenate([feats, side, jnp.zeros((56, TILE), F32)], axis=0).astype(BF16)
    cr[...] = jnp.concatenate(
        [jnp.zeros((64, TILE), F32), jnp.where(at8 == 6, alpha, 0.0), weight * probes,
         jnp.zeros((24, TILE), F32)], axis=0).astype(BF16)
    xct[:, 0:128] = jnp.concatenate([feats, feats], axis=0).T.astype(BF16)

    low = lax.broadcasted_iota(jnp.int32, (ITEM, 128), 1) < 64

    def products(r):
        cross = jnp.dot(r, cx[...], preferred_element_type=F32)
        weights = jnp.dot(r, cr[...], preferred_element_type=F32)
        prod = (weights * jnp.exp(cross)).astype(BF16)
        out = jnp.dot(prod, xct[...], preferred_element_type=F32)
        acc_col[...] += jnp.dot(r.T[0:80], prod, preferred_element_type=F32)
        return out

    def pack(out, r):
        def pick(v, k):
            return v.reshape(2 * ITEM // HALF, 2, 8, 128)[:, k].reshape(ITEM, 128)

        wide = r.astype(F32)
        feats = jnp.where(low, pick(wide, 0), pltpu.roll(pick(wide, 1), 64, axis=1))
        toward, total = out[:, :128], out[:, 128:]
        return (jnp.where(low, pick(toward, 0), pick(toward, 1))
                - jnp.where(low, pick(total, 0), pick(total, 1)) * feats)

    def core_copy(t, d):
        return pltpu.make_async_remote_copy(
            src_ref=core_out.at[t, d], dst_ref=core_in.at[t, d],
            send_sem=core_s.at[t, d], recv_sem=core_r.at[t, d], device_id=sibling, device_id_type=MESH)

    def part_copy(t, d):
        return pltpu.make_async_remote_copy(
            src_ref=axis_out.at[t, d], dst_ref=axis_in.at[t, d],
            send_sem=axis_s.at[t, d], recv_sem=axis_r.at[t, d], device_id=axis_peer(t, d), device_id_type=MESH)

    def pairs(s):
        return [[look([o[k][i] for o in STEPS], s) for i in range(2)] for k in range(2)]

    def some(table, s):
        return look([table.get(k, -1) for k in range(len(STEPS))], s)

    def begin(s, two, dc):
        passed = some(PASS_ON, s)

        @pl.when(passed >= 0)
        def _():
            for t, d in pairs(passed):
                g_copy(t, group(t, d, 0), sibling, f_s.at[t, 0]).wait_recv()
                sibling_copy(t, d).start()

        @pl.when(dc == 1)
        def _():
            for t, d in two:
                g_copy(t, group(t, d, 1), sibling, f_s.at[t, 0]).wait_recv()

    def end(packed, s, two, dc):
        half = ITEM // 2
        added = some(ADD_UP, s)

        @pl.when(dc == 0)
        def _():
            for k, (t, d) in enumerate(two):
                keep[t, d] = packed[k * half:(k + 1) * half]

        @pl.when(dc == 1)
        def _():
            for k, (t, d) in enumerate(two):
                core_out[t, d] = packed[k * half:(k + 1) * half].astype(BF16)
                core_copy(t, d).start()

        @pl.when(added >= 0)
        def _():
            for t, d in pairs(added):
                core_copy(t, d).wait_recv()
                axis_out[t, d] = (keep[t, d] + core_in[t, d].astype(F32)).astype(BF16)
                part_copy(t, d).start()

    def step(s, _):
        two, dc = pairs(s), look([o[2] for o in STEPS], s)

        @pl.when(s == 1)
        def _():
            for t in range(2):
                axis_copy(t, 2).start()

        begin(s, two, dc)
        r = jnp.concatenate([rows[t, group(t, d, dc)].reshape(ITEM, 128) for t, d in two], axis=0)
        end(pack(products(r), r), s, two, dc)
        return 0

    lax.fori_loop(0, len(STEPS), step, 0)

    grad = (acc_col[0:64] - acc_col[64:65] * cx[0:64].astype(F32)) * col_scale
    for p in range(8):
        block = grad[8 * p:8 * p + 8]
        back_out[p] = jnp.concatenate([block[:, :512], block[:, 512:]], axis=0).astype(BF16)
    back_start, back_forward, back_finish, back_sent = exchange(back_out, back_in, back_relay, back_s, back_r)
    back_start()

    def mm_copy(t, d):
        return pltpu.make_async_remote_copy(
            src_ref=mid_out.at[t, (place[t] + d) % 4], dst_ref=mid_in.at[t, d],
            send_sem=mm_s.at[t, d], recv_sem=mm_r.at[t, d], device_id=axis_peer(1 - t, d), device_id_type=MESH)

    mm_copies = []
    for t in range(2):
        core_copy(t, 0).wait_recv()
        total = keep[t, 0] + core_in[t, 0].astype(F32)
        for d in range(1, 4):
            part_copy(t, d).wait_recv()
            total += axis_in[t, d].astype(F32)
        keep[t, 0] = total
        mid_out[t] = total.reshape(4, 64, 128).astype(BF16)
        mm_copies.append([mm_copy(t, d) for d in FAR])
        for c in mm_copies[t]:
            c.start()

    blocks = []
    for t in range(2):
        total = keep[t, 0, pl.ds(pl.multiple_of(place[t] * 64, 64), 64), :]
        for c, d in zip(mm_copies[t], FAR):
            c.wait_recv()
            total += mid_in[t, d].astype(F32)
        blocks.append(total.reshape(NZ, 8, 128))
    z_out[...] = jnp.concatenate(blocks, axis=1).astype(BF16)

    def zz_copy(d):
        return pltpu.make_async_remote_copy(
            src_ref=z_out.at[(z + d) % NZ], dst_ref=z_in.at[d],
            send_sem=zz_s.at[d], recv_sem=zz_r.at[d], device_id=z_peer(d), device_id_type=MESH)

    zz_copies = [zz_copy(d) for d in FAR_Z]
    for c in zz_copies:
        c.start()
    mine = pltpu.make_async_copy(z_out.at[z], z_in.at[0], zz_s.at[0])
    mine.start()
    back_forward(0, 3)
    for c in zz_copies:
        c.wait_recv()
    mine.wait()
    back_finish()

    col_sent()
    back_sent()
    for c in z_copies + m_copies[0] + m_copies[1] + mm_copies[0] + mm_copies[1] + zz_copies:
        c.wait_send()
    for t in range(2):
        for d in range(4):
            sibling_copy(t, d).wait_send()
            core_copy(t, d).wait_send()
            if d:
                axis_copy(t, d).wait_send()
                part_copy(t, d).wait_send()


def unpack(row_scale, rows_ref, cols_ref, out_rows, out_cols):
    total = rows_ref[0].astype(F32)
    for d in range(1, NZ):
        total += rows_ref[d].astype(F32)
    total = total * row_scale
    moved = pltpu.roll(total, 64, axis=1)
    final = jnp.concatenate([total[0:8], moved[0:8], total[8:16], moved[8:16]], axis=0)
    out_rows[...] = final[:, 0:64]
    for p in range(8):
        block = cols_ref[p].astype(F32)
        out_cols[:, p * TILE:p * TILE + 512] = block[0:8]
        out_cols[:, p * TILE + 512:(p + 1) * TILE] = block[8:16]


def body(row_feats, row_alpha, row_solves, col_feats, col_alpha, col_weight, col_probes):
    row_size = lax.axis_size("row")
    col_size = lax.axis_size("col")
    own_rows = row_alpha.shape[0]
    own_cols = col_alpha.shape[0]
    window = own_rows * row_size * col_size
    points = own_cols * col_size
    dma = pltpu.SemaphoreType.DMA
    vmem = pl.BlockSpec(memory_space=pltpu.VMEM)
    hbm = pl.BlockSpec(memory_space=pltpu.HBM)
    args = (
        row_feats.T, row_alpha.reshape(1, -1), row_solves, col_feats,
        col_alpha.reshape(-1, 128), col_weight.reshape(-1, 128), col_probes,
    )
    half = ITEM // 2
    totals = pl.pallas_call(
        functools.partial(kernel, 1.0 / window**0.5),
        out_shape=(
            jax.ShapeDtypeStruct((NZ, 16, 128), BF16),
            jax.ShapeDtypeStruct((8, 16, 512), BF16),
        ),
        in_specs=[hbm] * 7,
        out_specs=(hbm, hbm),
        scratch_shapes=[
            *[pltpu.VMEM(a.shape, a.dtype) for a in args],
            dma((7,)),
            pltpu.VMEM((NZ, 2 * HALF, 128), BF16),
            pltpu.VMEM((2, 8, 4, NZ, HALF, 128), BF16),
            pltpu.VMEM((8, 16, 768), BF16),
            pltpu.VMEM((8, 16, 768), BF16),
            pltpu.VMEM((4, 16, 768), BF16),
            pltpu.VMEM((128, TILE), BF16),
            pltpu.VMEM((128, TILE), BF16),
            pltpu.VMEM((TILE, 256), BF16),
            pltpu.VMEM((own_cols // 128, 128), F32),
            pltpu.VMEM((80, TILE), F32),
            pltpu.VMEM((2, 4, half, 128), F32),
            *[pltpu.VMEM((2, 4, half, 128), BF16)] * 4,
            *[pltpu.VMEM((2, 4, half // 4, 128), BF16)] * 2,
            pltpu.VMEM((NZ, 16, 128), BF16),
            pltpu.VMEM((8, 16, 512), BF16),
            pltpu.VMEM((4, 16, 512), BF16),
            dma((3, 4)), dma((3, 4)), dma((NZ,)), dma((NZ,)), dma((2, 4)), dma((2, 4)),
            dma((2, 4)), dma((2, 8)), dma((2, 4)),
            *[dma((2, 4))] * 6,
            dma((NZ,)), dma((NZ,)), dma((3, 4)), dma((3, 4)),
        ],
        compiler_params=pltpu.CompilerParams(
            collective_id=0, has_side_effects=True, vmem_limit_bytes=63 * 2**20),
        name="evidence_gradients",
    )(*args)
    grad_rows, grad_cols = pl.pallas_call(
        functools.partial(unpack, 1.0 / points**0.5),
        out_shape=(
            jax.ShapeDtypeStruct((own_rows, FEAT), F32),
            jax.ShapeDtypeStruct((FEAT // row_size, own_cols), F32),
        ),
        in_specs=[vmem] * 2,
        out_specs=(vmem, vmem),
        name="unpack_gradients",
    )(*totals)
    return grad_rows.T, grad_cols


def solution(mesh):
    in_specs = (
        P(None, ("row", "col")),
        P(("row", "col")),
        P(None, ("row", "col")),
        P("row", "col"),
        P("col"),
        P("col"),
        P("row", "col"),
    )
    out_specs = (P(None, ("row", "col")), P("row", "col"))
    return jax.shard_map(body, mesh=mesh, in_specs=in_specs, out_specs=out_specs, check_vma=False)
```

```python
import functools

import jax
import jax.numpy as jnp
from jax import lax
from jax.experimental import pallas as pl
from jax.experimental.pallas import tpu as pltpu
from jax.sharding import PartitionSpec as P

MESH = pl.DeviceIdType.MESH
F32 = jnp.float32
FAR = (2, 1, 3)
FAR_Z = (4, 3, 5, 2, 6, 1, 7)
BF16 = jnp.bfloat16

FEAT = 64
PROBES = 32
NX, NY, NZ = 4, 4, 8
TILE = 1024
ITEM = 512
HALF = 16

STEPS = (
    ((0, 0), (1, 0), 1),
    ((0, 1), (0, 3), 0),
    ((0, 1), (0, 3), 1),
    ((1, 1), (1, 3), 1),
    ((0, 2), (1, 2), 1),
    ((0, 2), (1, 2), 0),
    ((1, 1), (1, 3), 0),
    ((0, 0), (1, 0), 0),
)
PASS_ON = {1: 1, 2: 6, 3: 5}
ADD_UP = {3: 1, 5: 5, 6: 6}


def look(values, at):
    out = jnp.int32(values[0])
    for k, v in enumerate(values[1:], 1):
        out = jnp.where(at == k, jnp.int32(v), out)
    return out


def parts3(v):
    hi = v.astype(BF16).astype(F32)
    mid = (v - hi).astype(BF16).astype(F32)
    return hi, mid, v - hi - mid


def kernel(
    col_scale,
    rf_hbm, ra_hbm, rs_hbm, cf_hbm, ca_hbm, cw_hbm, cp_hbm,
    z_in, back_in,
    rf_ref, ra_ref, rs_ref, cf_ref, ca_ref, cw_ref, cp_ref, in_s,
    zbuf, rows, send_cols, recv_cols, relay, cx, cr, xct, small, acc_col,
    keep, core_out, core_in, axis_out, axis_in,
    mid_out, mid_in, z_out, back_out, back_relay,
    col_s, col_r, z_s, z_r, m_s, m_r, g_s, g_r, f_s,
    core_s, core_r, axis_s, axis_r, mm_s, mm_r, zz_s, zz_r, back_s, back_r,
):
    row = lax.axis_index("row")
    col = lax.axis_index("col")
    y, core = row % 4, col % 2
    x, z = col // 8, (row // 4) * 4 + (col // 2) % 4

    def at(px, py, pz, pc):
        return {"row": (pz // 4) * 4 + py, "col": (px * 4 + pz % 4) * 2 + pc}

    def z_peer(d):
        return at(x, y, (z + d) % NZ, core)

    def axis_peer(t, d):
        return at((x + jnp.where(t == 0, d, 0)) % NX, (y + jnp.where(t == 1, d, 0)) % NY, z, core)

    sibling = at(x, y, z, 1 - core)
    far = (row + 4) % 8

    def row_of(d, other):
        return ((row // 4 + other) % 2) * 4 + (y + d) % 4

    def exchange(out, into, through, send, recv):
        def over_z(d):
            return pltpu.make_async_remote_copy(
                src_ref=out.at[row_of(d, 1)], dst_ref=through.at[d] if d else into.at[row],
                send_sem=send.at[0, d], recv_sem=recv.at[0, d], device_id=z_peer(4), device_id_type=MESH)

        def over_y(d):
            return pltpu.make_async_remote_copy(
                src_ref=out.at[row_of(d, 0)], dst_ref=into.at[row],
                send_sem=send.at[1, d], recv_sem=recv.at[1, d], device_id=axis_peer(1, d), device_id_type=MESH)

        def onward(d):
            return pltpu.make_async_remote_copy(
                src_ref=through.at[d], dst_ref=into.at[far],
                send_sem=send.at[2, d], recv_sem=recv.at[2, d], device_id=axis_peer(1, d), device_id_type=MESH)

        first = [over_z(d) for d in (2, 1, 3, 0)]
        second = [over_y(d) for d in (2, 1, 3)]
        third = [onward(d) for d in (2, 1, 3)]

        mine = pltpu.make_async_copy(out.at[row], into.at[row], send.at[1, 0])

        def start():
            for c in first + second:
                c.start()
            mine.start()

        def forward(begin, end):
            for a, b in zip(first[begin:end], third[begin:end]):
                a.wait_recv()
                b.start()

        def finish():
            for c in second + [first[3]] + third:
                c.wait_recv()
            mine.wait()

        def sent():
            for c in first + second + third:
                c.wait_send()

        return start, forward, finish, sent

    loads = [
        pltpu.make_async_copy(src, dst, in_s.at[k])
        for k, (src, dst) in enumerate((
            (rf_hbm, rf_ref), (ra_hbm, ra_ref), (rs_hbm, rs_ref), (cf_hbm, cf_ref),
            (cp_hbm, cp_ref), (ca_hbm, ca_ref), (cw_hbm, cw_ref)))
    ]
    barrier = pltpu.get_barrier_semaphore()
    peers = [z_peer(d) for d in FAR_Z]
    peers += [axis_peer(t, d) for t in range(2) for d in FAR] + [sibling]
    for peer in peers:
        pl.semaphore_signal(barrier, inc=1, device_id=peer, device_id_type=MESH)
    for c in loads:
        c.start()

    for c in loads[:3]:
        c.wait()
    n = 2 * HALF
    rf = rf_ref[...].astype(F32)
    sq = -0.5 * jnp.sum(rf * rf, axis=1, keepdims=True)
    at8 = lax.broadcasted_iota(jnp.int32, (8, n), 0)
    side = jnp.concatenate(
        [jnp.zeros((64, n), F32), jnp.where(at8 == 6, ra_ref[...].astype(F32), 0.0),
         rs_ref[...].astype(F32), jnp.zeros((24, n), F32)], axis=0)
    side = jnp.concatenate([side, jnp.zeros((128, 128 - n), F32)], axis=1).T[:n]
    lane = lax.broadcasted_iota(jnp.int32, (n, 128), 1)
    mine = side + jnp.concatenate([rf, jnp.zeros((n, 64), F32)], axis=1)
    mine = jnp.where(jnp.logical_and(lane >= 64, lane < 67), 1.0, mine)
    for k, v in enumerate(parts3(sq)):
        mine = jnp.where(lane == 67 + k, v, mine)
    zbuf[z] = mine.astype(BF16)

    for c in loads[3:5]:
        c.wait()
    for p in range(8):
        span = slice(p * TILE, (p + 1) * TILE)
        feats = cf_ref[:, span].astype(F32)
        probes = cp_ref[:, span].astype(F32)
        left = jnp.concatenate([feats[:, :512], feats[:, 512:]], axis=0)
        right = jnp.concatenate([probes[:, q * 256:(q + 1) * 256] for q in range(4)], axis=0)
        send_cols[p] = jnp.concatenate([left, right], axis=1).astype(BF16)

    for c in loads[5:]:
        c.wait()
    eight = pl.ds(pl.multiple_of(row * 8, 8), 8)
    weight = cw_ref[eight, :]
    small[...] = ca_ref[...].astype(F32)
    alpha = small[eight, :]
    weight = jnp.concatenate([weight[k:k + 1] for k in range(8)], axis=1) * (-0.5 / PROBES)
    alpha = jnp.concatenate([alpha[k:k + 1] for k in range(8)], axis=1) * 0.5
    xct[:, 128:] = jnp.ones((TILE, 128), BF16)
    acc_col[...] = jnp.zeros_like(acc_col)

    pl.semaphore_wait(barrier, len(peers))

    def z_copy(d):
        return pltpu.make_async_remote_copy(
            src_ref=zbuf.at[z], dst_ref=zbuf.at[z],
            send_sem=z_s.at[d], recv_sem=z_r.at[d], device_id=z_peer(d), device_id_type=MESH)

    own = (x * 2 + core, y * 2 + core)
    place = (y, x)

    def m_copy(t, d):
        return pltpu.make_async_remote_copy(
            src_ref=rows.at[t, own[t], place[t]], dst_ref=rows.at[t, own[t], place[t]],
            send_sem=m_s.at[t, d], recv_sem=m_r.at[t, d], device_id=axis_peer(1 - t, d), device_id_type=MESH)

    def g_copy(t, g, peer, send_sem):
        return pltpu.make_async_remote_copy(
            src_ref=rows.at[t, g], dst_ref=rows.at[t, g],
            send_sem=send_sem, recv_sem=g_r.at[t, g], device_id=peer, device_id_type=MESH)

    def group(t, d, dc):
        return jnp.where(t == 0, (x + d) % NX, (y + d) % NY) * 2 + (core + dc) % 2

    def axis_copy(t, d):
        return g_copy(t, group(t, 0, 0), axis_peer(t, d), g_s.at[t, d])

    def sibling_copy(t, d):
        return g_copy(t, group(t, d, 0), sibling, f_s.at[t, d])

    z_copies = [z_copy(d) for d in FAR_Z]
    for c in z_copies:
        c.start()
    col_start, col_forward, col_finish, col_sent = exchange(send_cols, recv_cols, relay, col_s, col_r)
    col_start()
    for c in z_copies:
        c.wait_recv()
    m_copies = [None, None]
    for t in (1, 0):
        rows[t, own[t], place[t]] = zbuf[:, t * HALF:(t + 1) * HALF]
        m_copies[t] = [m_copy(t, d) for d in FAR]
        for c in m_copies[t]:
            c.start()
    col_forward(0, 3)
    for t in range(2):
        for c in m_copies[t]:
            c.wait_recv()
        sibling_copy(t, 0).start()
    for d in (1, 3):
        axis_copy(0, d).start()
    for d in (1, 3):
        axis_copy(1, d).start()
    col_finish()

    feats = jnp.concatenate(
        [jnp.concatenate([recv_cols[p, :, 0:512].astype(F32)[8 * k:8 * k + 8] for k in range(2)], axis=1)
         for p in range(8)], axis=0)
    probes = []
    for p in range(8):
        block = recv_cols[p, :, 512:768].astype(F32)
        probes.append(jnp.concatenate([block[4 * q:4 * q + 4] for q in range(4)], axis=1))
    probes = jnp.concatenate(probes, axis=0)
    sq = parts3(-0.5 * jnp.sum(feats * feats, axis=0, keepdims=True))
    at8 = lax.broadcasted_iota(jnp.int32, (8, TILE), 0)
    side = jnp.where(at8 < 6, 1.0, 0.0)
    for k, v in enumerate(sq):
        side = jnp.where(at8 == k, v, side)
    cx[...] = jnp.concatenate([feats, side, jnp.zeros((56, TILE), F32)], axis=0).astype(BF16)
    cr[...] = jnp.concatenate(
        [jnp.zeros((64, TILE), F32), jnp.where(at8 == 6, alpha, 0.0), weight * probes,
         jnp.zeros((24, TILE), F32)], axis=0).astype(BF16)
    xct[:, 0:128] = jnp.concatenate([feats, feats], axis=0).T.astype(BF16)

    low = lax.broadcasted_iota(jnp.int32, (ITEM, 128), 1) < 64

    def products(r):
        cross = jnp.dot(r, cx[...], preferred_element_type=F32)
        weights = jnp.dot(r, cr[...], preferred_element_type=F32)
        prod = (weights * jnp.exp(cross)).astype(BF16)
        out = jnp.dot(prod, xct[...], preferred_element_type=F32)
        acc_col[...] += jnp.dot(r.T[0:80], prod, preferred_element_type=F32)
        return out

    def pack(out, r):
        def pick(v, k):
            return v.reshape(2 * ITEM // HALF, 2, 8, 128)[:, k].reshape(ITEM, 128)

        wide = r.astype(F32)
        feats = jnp.where(low, pick(wide, 0), pltpu.roll(pick(wide, 1), 64, axis=1))
        toward, total = out[:, :128], out[:, 128:]
        return (jnp.where(low, pick(toward, 0), pick(toward, 1))
                - jnp.where(low, pick(total, 0), pick(total, 1)) * feats)

    def core_copy(t, d):
        return pltpu.make_async_remote_copy(
            src_ref=core_out.at[t, d], dst_ref=core_in.at[t, d],
            send_sem=core_s.at[t, d], recv_sem=core_r.at[t, d], device_id=sibling, device_id_type=MESH)

    def part_copy(t, d):
        return pltpu.make_async_remote_copy(
            src_ref=axis_out.at[t, d], dst_ref=axis_in.at[t, d],
            send_sem=axis_s.at[t, d], recv_sem=axis_r.at[t, d], device_id=axis_peer(t, d), device_id_type=MESH)

    def pairs(s):
        return [[look([o[k][i] for o in STEPS], s) for i in range(2)] for k in range(2)]

    def some(table, s):
        return look([table.get(k, -1) for k in range(len(STEPS))], s)

    def begin(s, two, dc):
        passed = some(PASS_ON, s)

        @pl.when(passed >= 0)
        def _():
            for t, d in pairs(passed):
                g_copy(t, group(t, d, 0), sibling, f_s.at[t, 0]).wait_recv()
                sibling_copy(t, d).start()

        @pl.when(dc == 1)
        def _():
            for t, d in two:
                g_copy(t, group(t, d, 1), sibling, f_s.at[t, 0]).wait_recv()

    def end(packed, s, two, dc):
        half = ITEM // 2
        added = some(ADD_UP, s)

        @pl.when(dc == 0)
        def _():
            for k, (t, d) in enumerate(two):
                keep[t, d] = packed[k * half:(k + 1) * half]

        @pl.when(dc == 1)
        def _():
            for k, (t, d) in enumerate(two):
                core_out[t, d] = packed[k * half:(k + 1) * half].astype(BF16)
                core_copy(t, d).start()

        @pl.when(added >= 0)
        def _():
            for t, d in pairs(added):
                core_copy(t, d).wait_recv()
                axis_out[t, d] = (keep[t, d] + core_in[t, d].astype(F32)).astype(BF16)
                part_copy(t, d).start()

    def step(s, _):
        two, dc = pairs(s), look([o[2] for o in STEPS], s)

        @pl.when(s == 1)
        def _():
            for t in range(2):
                axis_copy(t, 2).start()

        begin(s, two, dc)
        r = jnp.concatenate([rows[t, group(t, d, dc)].reshape(ITEM, 128) for t, d in two], axis=0)
        end(pack(products(r), r), s, two, dc)
        return 0

    lax.fori_loop(0, len(STEPS), step, 0)

    grad = (acc_col[0:64] - acc_col[64:65] * cx[0:64].astype(F32)) * col_scale
    for p in range(8):
        block = grad[8 * p:8 * p + 8]
        back_out[p] = jnp.concatenate([block[:, :512], block[:, 512:]], axis=0).astype(BF16)
    back_start, back_forward, back_finish, back_sent = exchange(back_out, back_in, back_relay, back_s, back_r)
    back_start()

    def mm_copy(t, d):
        return pltpu.make_async_remote_copy(
            src_ref=mid_out.at[t, (place[t] + d) % 4], dst_ref=mid_in.at[t, d],
            send_sem=mm_s.at[t, d], recv_sem=mm_r.at[t, d], device_id=axis_peer(1 - t, d), device_id_type=MESH)

    mm_copies = []
    for t in range(2):
        core_copy(t, 0).wait_recv()
        total = keep[t, 0] + core_in[t, 0].astype(F32)
        for d in range(1, 4):
            part_copy(t, d).wait_recv()
            total += axis_in[t, d].astype(F32)
        keep[t, 0] = total
        mid_out[t] = total.reshape(4, 64, 128).astype(BF16)
        mm_copies.append([mm_copy(t, d) for d in FAR])
        for c in mm_copies[t]:
            c.start()

    blocks = []
    for t in range(2):
        total = keep[t, 0, pl.ds(pl.multiple_of(place[t] * 64, 64), 64), :]
        for c, d in zip(mm_copies[t], FAR):
            c.wait_recv()
            total += mid_in[t, d].astype(F32)
        blocks.append(total.reshape(NZ, 8, 128))
    z_out[...] = jnp.concatenate(blocks, axis=1).astype(BF16)

    def zz_copy(d):
        return pltpu.make_async_remote_copy(
            src_ref=z_out.at[(z + d) % NZ], dst_ref=z_in.at[d],
            send_sem=zz_s.at[d], recv_sem=zz_r.at[d], device_id=z_peer(d), device_id_type=MESH)

    zz_copies = [zz_copy(d) for d in FAR_Z]
    for c in zz_copies:
        c.start()
    mine = pltpu.make_async_copy(z_out.at[z], z_in.at[0], zz_s.at[0])
    mine.start()
    back_forward(0, 3)
    for c in zz_copies:
        c.wait_recv()
    mine.wait()
    back_finish()

    col_sent()
    back_sent()
    for c in z_copies + m_copies[0] + m_copies[1] + mm_copies[0] + mm_copies[1] + zz_copies:
        c.wait_send()
    for t in range(2):
        for d in range(4):
            sibling_copy(t, d).wait_send()
            core_copy(t, d).wait_send()
            if d:
                axis_copy(t, d).wait_send()
                part_copy(t, d).wait_send()


def unpack(row_scale, rows_ref, cols_ref, out_rows, out_cols):
    total = rows_ref[0].astype(F32)
    for d in range(1, NZ):
        total += rows_ref[d].astype(F32)
    total = total * row_scale
    moved = pltpu.roll(total, 64, axis=1)
    final = jnp.concatenate([total[0:8], moved[0:8], total[8:16], moved[8:16]], axis=0)
    out_rows[...] = final[:, 0:64]
    for p in range(8):
        block = cols_ref[p].astype(F32)
        out_cols[:, p * TILE:p * TILE + 512] = block[0:8]
        out_cols[:, p * TILE + 512:(p + 1) * TILE] = block[8:16]


def body(row_feats, row_alpha, row_solves, col_feats, col_alpha, col_weight, col_probes):
    row_size = lax.axis_size("row")
    col_size = lax.axis_size("col")
    own_rows = row_alpha.shape[0]
    own_cols = col_alpha.shape[0]
    window = own_rows * row_size * col_size
    points = own_cols * col_size
    dma = pltpu.SemaphoreType.DMA
    vmem = pl.BlockSpec(memory_space=pltpu.VMEM)
    hbm = pl.BlockSpec(memory_space=pltpu.HBM)
    args = (
        row_feats.T, row_alpha.reshape(1, -1), row_solves, col_feats,
        col_alpha.reshape(-1, 128), col_weight.reshape(-1, 128), col_probes,
    )
    half = ITEM // 2
    totals = pl.pallas_call(
        functools.partial(kernel, 1.0 / window**0.5),
        out_shape=(
            jax.ShapeDtypeStruct((NZ, 16, 128), BF16),
            jax.ShapeDtypeStruct((8, 16, 512), BF16),
        ),
        in_specs=[hbm] * 7,
        out_specs=(hbm, hbm),
        scratch_shapes=[
            *[pltpu.VMEM(a.shape, a.dtype) for a in args],
            dma((7,)),
            pltpu.VMEM((NZ, 2 * HALF, 128), BF16),
            pltpu.VMEM((2, 8, 4, NZ, HALF, 128), BF16),
            pltpu.VMEM((8, 16, 768), BF16),
            pltpu.VMEM((8, 16, 768), BF16),
            pltpu.VMEM((4, 16, 768), BF16),
            pltpu.VMEM((128, TILE), BF16),
            pltpu.VMEM((128, TILE), BF16),
            pltpu.VMEM((TILE, 256), BF16),
            pltpu.VMEM((own_cols // 128, 128), F32),
            pltpu.VMEM((80, TILE), F32),
            pltpu.VMEM((2, 4, half, 128), F32),
            *[pltpu.VMEM((2, 4, half, 128), BF16)] * 4,
            *[pltpu.VMEM((2, 4, half // 4, 128), BF16)] * 2,
            pltpu.VMEM((NZ, 16, 128), BF16),
            pltpu.VMEM((8, 16, 512), BF16),
            pltpu.VMEM((4, 16, 512), BF16),
            dma((3, 4)), dma((3, 4)), dma((NZ,)), dma((NZ,)), dma((2, 4)), dma((2, 4)),
            dma((2, 4)), dma((2, 8)), dma((2, 4)),
            *[dma((2, 4))] * 6,
            dma((NZ,)), dma((NZ,)), dma((3, 4)), dma((3, 4)),
        ],
        compiler_params=pltpu.CompilerParams(
            collective_id=0, has_side_effects=True, vmem_limit_bytes=63 * 2**20),
        name="evidence_gradients",
    )(*args)
    grad_rows, grad_cols = pl.pallas_call(
        functools.partial(unpack, 1.0 / points**0.5),
        out_shape=(
            jax.ShapeDtypeStruct((own_rows, FEAT), F32),
            jax.ShapeDtypeStruct((FEAT // row_size, own_cols), F32),
        ),
        in_specs=[vmem] * 2,
        out_specs=(vmem, vmem),
        name="unpack_gradients",
    )(*totals)
    return grad_rows.T, grad_cols


def solution(mesh):
    in_specs = (
        P(None, ("row", "col")),
        P(("row", "col")),
        P(None, ("row", "col")),
        P("row", "col"),
        P("col"),
        P("col"),
        P("row", "col"),
    )
    out_specs = (P(None, ("row", "col")), P("row", "col"))
    return jax.shard_map(body, mesh=mesh, in_specs=in_specs, out_specs=out_specs, check_vma=False)
```

```python
import functools

import jax
import jax.numpy as jnp
from jax import lax
from jax.experimental import pallas as pl
from jax.experimental.pallas import tpu as pltpu
from jax.sharding import PartitionSpec as P

MESH = pl.DeviceIdType.MESH
F32 = jnp.float32
FAR = (2, 1, 3)
FAR_Z = (4, 3, 5, 2, 6, 1, 7)
BF16 = jnp.bfloat16

FEAT = 64
PROBES = 32
NX, NY, NZ = 4, 4, 8
TILE = 1024
ITEM = 512
HALF = 16

STEPS = (
    ((0, 0), (1, 0), 1),
    ((0, 1), (0, 3), 0),
    ((0, 1), (0, 3), 1),
    ((1, 1), (1, 3), 1),
    ((0, 2), (1, 2), 1),
    ((0, 2), (1, 2), 0),
    ((1, 1), (1, 3), 0),
    ((0, 0), (1, 0), 0),
)
PASS_ON = {1: 1, 2: 6, 3: 5}
ADD_UP = {3: 1, 5: 5, 6: 6}


def look(values, at):
    out = jnp.int32(values[0])
    for k, v in enumerate(values[1:], 1):
        out = jnp.where(at == k, jnp.int32(v), out)
    return out


def parts3(v):
    hi = v.astype(BF16).astype(F32)
    mid = (v - hi).astype(BF16).astype(F32)
    return hi, mid, v - hi - mid


def kernel(
    col_scale,
    rf_hbm, ra_hbm, rs_hbm, cf_hbm, ca_hbm, cw_hbm, cp_hbm,
    z_in, back_in,
    rf_ref, ra_ref, rs_ref, cf_ref, ca_ref, cw_ref, cp_ref, in_s,
    zbuf, rows, send_cols, recv_cols, relay, cx, cr, xct, small, acc_col,
    keep, core_out, core_in, axis_out, axis_in,
    mid_out, mid_in, z_out, back_out, back_relay,
    col_s, col_r, z_s, z_r, m_s, m_r, g_s, g_r, f_s,
    core_s, core_r, axis_s, axis_r, mm_s, mm_r, zz_s, zz_r, back_s, back_r,
):
    row = lax.axis_index("row")
    col = lax.axis_index("col")
    y, core = row % 4, col % 2
    x, z = col // 8, (row // 4) * 4 + (col // 2) % 4

    def at(px, py, pz, pc):
        return {"row": (pz // 4) * 4 + py, "col": (px * 4 + pz % 4) * 2 + pc}

    def z_peer(d):
        return at(x, y, (z + d) % NZ, core)

    def axis_peer(t, d):
        return at((x + jnp.where(t == 0, d, 0)) % NX, (y + jnp.where(t == 1, d, 0)) % NY, z, core)

    sibling = at(x, y, z, 1 - core)
    far = (row + 4) % 8

    def row_of(d, other):
        return ((row // 4 + other) % 2) * 4 + (y + d) % 4

    def exchange(out, into, through, send, recv):
        def over_z(d):
            return pltpu.make_async_remote_copy(
                src_ref=out.at[row_of(d, 1)], dst_ref=through.at[d] if d else into.at[row],
                send_sem=send.at[0, d], recv_sem=recv.at[0, d], device_id=z_peer(4), device_id_type=MESH)

        def over_y(d):
            return pltpu.make_async_remote_copy(
                src_ref=out.at[row_of(d, 0)], dst_ref=into.at[row],
                send_sem=send.at[1, d], recv_sem=recv.at[1, d], device_id=axis_peer(1, d), device_id_type=MESH)

        def onward(d):
            return pltpu.make_async_remote_copy(
                src_ref=through.at[d], dst_ref=into.at[far],
                send_sem=send.at[2, d], recv_sem=recv.at[2, d], device_id=axis_peer(1, d), device_id_type=MESH)

        first = [over_z(d) for d in (2, 1, 3, 0)]
        second = [over_y(d) for d in (2, 1, 3)]
        third = [onward(d) for d in (2, 1, 3)]

        mine = pltpu.make_async_copy(out.at[row], into.at[row], send.at[1, 0])

        def start():
            for c in first:
                c.start()
            mine.start()

        def along_y():
            for c in second:
                c.start()

        def forward(begin, end):
            for a, b in zip(first[begin:end], third[begin:end]):
                a.wait_recv()
                b.start()

        def finish():
            for c in second + [first[3]] + third:
                c.wait_recv()
            mine.wait()

        def sent():
            for c in first + second + third:
                c.wait_send()

        return start, along_y, forward, finish, sent

    loads = [
        pltpu.make_async_copy(src, dst, in_s.at[k])
        for k, (src, dst) in enumerate((
            (rf_hbm, rf_ref), (ra_hbm, ra_ref), (rs_hbm, rs_ref), (cf_hbm, cf_ref),
            (cp_hbm, cp_ref), (ca_hbm, ca_ref), (cw_hbm, cw_ref)))
    ]
    barrier = pltpu.get_barrier_semaphore()
    peers = [z_peer(d) for d in FAR_Z]
    peers += [axis_peer(t, d) for t in range(2) for d in FAR] + [sibling]
    for peer in peers:
        pl.semaphore_signal(barrier, inc=1, device_id=peer, device_id_type=MESH)
    for c in loads:
        c.start()

    for c in loads[:3]:
        c.wait()
    n = 2 * HALF
    rf = rf_ref[...].astype(F32)
    sq = -0.5 * jnp.sum(rf * rf, axis=1, keepdims=True)
    at8 = lax.broadcasted_iota(jnp.int32, (8, n), 0)
    side = jnp.concatenate(
        [jnp.zeros((64, n), F32), jnp.where(at8 == 6, ra_ref[...].astype(F32), 0.0),
         rs_ref[...].astype(F32), jnp.zeros((24, n), F32)], axis=0)
    side = jnp.concatenate([side, jnp.zeros((128, 128 - n), F32)], axis=1).T[:n]
    lane = lax.broadcasted_iota(jnp.int32, (n, 128), 1)
    mine = side + jnp.concatenate([rf, jnp.zeros((n, 64), F32)], axis=1)
    mine = jnp.where(jnp.logical_and(lane >= 64, lane < 67), 1.0, mine)
    for k, v in enumerate(parts3(sq)):
        mine = jnp.where(lane == 67 + k, v, mine)
    zbuf[z] = mine.astype(BF16)

    for c in loads[3:5]:
        c.wait()
    for p in range(8):
        span = slice(p * TILE, (p + 1) * TILE)
        feats = cf_ref[:, span].astype(F32)
        probes = cp_ref[:, span].astype(F32)
        left = jnp.concatenate([feats[:, :512], feats[:, 512:]], axis=0)
        right = jnp.concatenate([probes[:, q * 256:(q + 1) * 256] for q in range(4)], axis=0)
        send_cols[p] = jnp.concatenate([left, right], axis=1).astype(BF16)

    for c in loads[5:]:
        c.wait()
    eight = pl.ds(pl.multiple_of(row * 8, 8), 8)
    weight = cw_ref[eight, :]
    small[...] = ca_ref[...].astype(F32)
    alpha = small[eight, :]
    weight = jnp.concatenate([weight[k:k + 1] for k in range(8)], axis=1) * (-0.5 / PROBES)
    alpha = jnp.concatenate([alpha[k:k + 1] for k in range(8)], axis=1) * 0.5
    xct[:, 128:] = jnp.ones((TILE, 128), BF16)
    acc_col[...] = jnp.zeros_like(acc_col)

    pl.semaphore_wait(barrier, len(peers))

    def z_copy(d):
        return pltpu.make_async_remote_copy(
            src_ref=zbuf.at[z], dst_ref=zbuf.at[z],
            send_sem=z_s.at[d], recv_sem=z_r.at[d], device_id=z_peer(d), device_id_type=MESH)

    own = (x * 2 + core, y * 2 + core)
    place = (y, x)

    def m_copy(t, d):
        return pltpu.make_async_remote_copy(
            src_ref=rows.at[t, own[t], place[t]], dst_ref=rows.at[t, own[t], place[t]],
            send_sem=m_s.at[t, d], recv_sem=m_r.at[t, d], device_id=axis_peer(1 - t, d), device_id_type=MESH)

    def g_copy(t, g, peer, send_sem):
        return pltpu.make_async_remote_copy(
            src_ref=rows.at[t, g], dst_ref=rows.at[t, g],
            send_sem=send_sem, recv_sem=g_r.at[t, g], device_id=peer, device_id_type=MESH)

    def group(t, d, dc):
        return jnp.where(t == 0, (x + d) % NX, (y + d) % NY) * 2 + (core + dc) % 2

    def axis_copy(t, d):
        return g_copy(t, group(t, 0, 0), axis_peer(t, d), g_s.at[t, d])

    def sibling_copy(t, d):
        return g_copy(t, group(t, d, 0), sibling, f_s.at[t, d])

    z_copies = [z_copy(d) for d in FAR_Z]
    for c in z_copies:
        c.start()
    col_start, col_along_y, col_forward, col_finish, col_sent = exchange(send_cols, recv_cols, relay, col_s, col_r)
    col_start()
    col_along_y()
    for c in z_copies:
        c.wait_recv()
    m_copies = [None, None]
    for t in (1, 0):
        rows[t, own[t], place[t]] = zbuf[:, t * HALF:(t + 1) * HALF]
        m_copies[t] = [m_copy(t, d) for d in FAR]
        for c in m_copies[t]:
            c.start()
    col_forward(0, 3)
    for t in range(2):
        for c in m_copies[t]:
            c.wait_recv()
        sibling_copy(t, 0).start()
    for d in (1, 3):
        axis_copy(0, d).start()
    for d in (1, 3):
        axis_copy(1, d).start()
    col_finish()

    feats = jnp.concatenate(
        [jnp.concatenate([recv_cols[p, :, 0:512].astype(F32)[8 * k:8 * k + 8] for k in range(2)], axis=1)
         for p in range(8)], axis=0)
    probes = []
    for p in range(8):
        block = recv_cols[p, :, 512:768].astype(F32)
        probes.append(jnp.concatenate([block[4 * q:4 * q + 4] for q in range(4)], axis=1))
    probes = jnp.concatenate(probes, axis=0)
    sq = parts3(-0.5 * jnp.sum(feats * feats, axis=0, keepdims=True))
    at8 = lax.broadcasted_iota(jnp.int32, (8, TILE), 0)
    side = jnp.where(at8 < 6, 1.0, 0.0)
    for k, v in enumerate(sq):
        side = jnp.where(at8 == k, v, side)
    cx[...] = jnp.concatenate([feats, side, jnp.zeros((56, TILE), F32)], axis=0).astype(BF16)
    cr[...] = jnp.concatenate(
        [jnp.zeros((64, TILE), F32), jnp.where(at8 == 6, alpha, 0.0), weight * probes,
         jnp.zeros((24, TILE), F32)], axis=0).astype(BF16)
    xct[:, 0:128] = jnp.concatenate([feats, feats], axis=0).T.astype(BF16)

    low = lax.broadcasted_iota(jnp.int32, (ITEM, 128), 1) < 64

    def products(r):
        cross = jnp.dot(r, cx[...], preferred_element_type=F32)
        weights = jnp.dot(r, cr[...], preferred_element_type=F32)
        prod = (weights * jnp.exp(cross)).astype(BF16)
        out = jnp.dot(prod, xct[...], preferred_element_type=F32)
        acc_col[...] += jnp.dot(r.T[0:80], prod, preferred_element_type=F32)
        return out

    def pack(out, r):
        def pick(v, k):
            return v.reshape(2 * ITEM // HALF, 2, 8, 128)[:, k].reshape(ITEM, 128)

        wide = r.astype(F32)
        feats = jnp.where(low, pick(wide, 0), pltpu.roll(pick(wide, 1), 64, axis=1))
        toward, total = out[:, :128], out[:, 128:]
        return (jnp.where(low, pick(toward, 0), pick(toward, 1))
                - jnp.where(low, pick(total, 0), pick(total, 1)) * feats)

    def core_copy(t, d):
        return pltpu.make_async_remote_copy(
            src_ref=core_out.at[t, d], dst_ref=core_in.at[t, d],
            send_sem=core_s.at[t, d], recv_sem=core_r.at[t, d], device_id=sibling, device_id_type=MESH)

    def part_copy(t, d):
        return pltpu.make_async_remote_copy(
            src_ref=axis_out.at[t, d], dst_ref=axis_in.at[t, d],
            send_sem=axis_s.at[t, d], recv_sem=axis_r.at[t, d], device_id=axis_peer(t, d), device_id_type=MESH)

    def pairs(s):
        return [[look([o[k][i] for o in STEPS], s) for i in range(2)] for k in range(2)]

    def some(table, s):
        return look([table.get(k, -1) for k in range(len(STEPS))], s)

    def begin(s, two, dc):
        passed = some(PASS_ON, s)

        @pl.when(passed >= 0)
        def _():
            for t, d in pairs(passed):
                g_copy(t, group(t, d, 0), sibling, f_s.at[t, 0]).wait_recv()
                sibling_copy(t, d).start()

        @pl.when(dc == 1)
        def _():
            for t, d in two:
                g_copy(t, group(t, d, 1), sibling, f_s.at[t, 0]).wait_recv()

    def end(packed, s, two, dc):
        half = ITEM // 2
        added = some(ADD_UP, s)

        @pl.when(dc == 0)
        def _():
            for k, (t, d) in enumerate(two):
                keep[t, d] = packed[k * half:(k + 1) * half]

        @pl.when(dc == 1)
        def _():
            for k, (t, d) in enumerate(two):
                core_out[t, d] = packed[k * half:(k + 1) * half].astype(BF16)
                core_copy(t, d).start()

        @pl.when(added >= 0)
        def _():
            for t, d in pairs(added):
                core_copy(t, d).wait_recv()
                axis_out[t, d] = (keep[t, d] + core_in[t, d].astype(F32)).astype(BF16)
                part_copy(t, d).start()

    def step(s, _):
        two, dc = pairs(s), look([o[2] for o in STEPS], s)

        @pl.when(s == 1)
        def _():
            for t in range(2):
                axis_copy(t, 2).start()

        begin(s, two, dc)
        r = jnp.concatenate([rows[t, group(t, d, dc)].reshape(ITEM, 128) for t, d in two], axis=0)
        end(pack(products(r), r), s, two, dc)
        return 0

    lax.fori_loop(0, len(STEPS), step, 0)

    grad = (acc_col[0:64] - acc_col[64:65] * cx[0:64].astype(F32)) * col_scale
    for p in range(8):
        block = grad[8 * p:8 * p + 8]
        back_out[p] = jnp.concatenate([block[:, :512], block[:, 512:]], axis=0).astype(BF16)
    back_start, back_along_y, back_forward, back_finish, back_sent = exchange(back_out, back_in, back_relay, back_s, back_r)
    back_start()

    def mm_copy(t, d):
        return pltpu.make_async_remote_copy(
            src_ref=mid_out.at[t, (place[t] + d) % 4], dst_ref=mid_in.at[t, d],
            send_sem=mm_s.at[t, d], recv_sem=mm_r.at[t, d], device_id=axis_peer(1 - t, d), device_id_type=MESH)

    mm_copies = []
    for t in range(2):
        core_copy(t, 0).wait_recv()
        total = keep[t, 0] + core_in[t, 0].astype(F32)
        for d in range(1, 4):
            part_copy(t, d).wait_recv()
            total += axis_in[t, d].astype(F32)
        keep[t, 0] = total
        mid_out[t] = total.reshape(4, 64, 128).astype(BF16)
        mm_copies.append([mm_copy(t, d) for d in FAR])
        for c in mm_copies[t]:
            c.start()

    back_along_y()
    blocks = []
    for t in range(2):
        total = keep[t, 0, pl.ds(pl.multiple_of(place[t] * 64, 64), 64), :]
        for c, d in zip(mm_copies[t], FAR):
            c.wait_recv()
            total += mid_in[t, d].astype(F32)
        blocks.append(total.reshape(NZ, 8, 128))
    z_out[...] = jnp.concatenate(blocks, axis=1).astype(BF16)

    def zz_copy(d):
        return pltpu.make_async_remote_copy(
            src_ref=z_out.at[(z + d) % NZ], dst_ref=z_in.at[d],
            send_sem=zz_s.at[d], recv_sem=zz_r.at[d], device_id=z_peer(d), device_id_type=MESH)

    zz_copies = [zz_copy(d) for d in FAR_Z]
    for c in zz_copies:
        c.start()
    mine = pltpu.make_async_copy(z_out.at[z], z_in.at[0], zz_s.at[0])
    mine.start()
    back_forward(0, 3)
    for c in zz_copies:
        c.wait_recv()
    mine.wait()
    back_finish()

    col_sent()
    back_sent()
    for c in z_copies + m_copies[0] + m_copies[1] + mm_copies[0] + mm_copies[1] + zz_copies:
        c.wait_send()
    for t in range(2):
        for d in range(4):
            sibling_copy(t, d).wait_send()
            core_copy(t, d).wait_send()
            if d:
                axis_copy(t, d).wait_send()
                part_copy(t, d).wait_send()


def unpack(row_scale, rows_ref, cols_ref, out_rows, out_cols):
    total = rows_ref[0].astype(F32)
    for d in range(1, NZ):
        total += rows_ref[d].astype(F32)
    total = total * row_scale
    moved = pltpu.roll(total, 64, axis=1)
    final = jnp.concatenate([total[0:8], moved[0:8], total[8:16], moved[8:16]], axis=0)
    out_rows[...] = final[:, 0:64]
    for p in range(8):
        block = cols_ref[p].astype(F32)
        out_cols[:, p * TILE:p * TILE + 512] = block[0:8]
        out_cols[:, p * TILE + 512:(p + 1) * TILE] = block[8:16]


def body(row_feats, row_alpha, row_solves, col_feats, col_alpha, col_weight, col_probes):
    row_size = lax.axis_size("row")
    col_size = lax.axis_size("col")
    own_rows = row_alpha.shape[0]
    own_cols = col_alpha.shape[0]
    window = own_rows * row_size * col_size
    points = own_cols * col_size
    dma = pltpu.SemaphoreType.DMA
    vmem = pl.BlockSpec(memory_space=pltpu.VMEM)
    hbm = pl.BlockSpec(memory_space=pltpu.HBM)
    args = (
        row_feats.T, row_alpha.reshape(1, -1), row_solves, col_feats,
        col_alpha.reshape(-1, 128), col_weight.reshape(-1, 128), col_probes,
    )
    half = ITEM // 2
    totals = pl.pallas_call(
        functools.partial(kernel, 1.0 / window**0.5),
        out_shape=(
            jax.ShapeDtypeStruct((NZ, 16, 128), BF16),
            jax.ShapeDtypeStruct((8, 16, 512), BF16),
        ),
        in_specs=[hbm] * 7,
        out_specs=(hbm, hbm),
        scratch_shapes=[
            *[pltpu.VMEM(a.shape, a.dtype) for a in args],
            dma((7,)),
            pltpu.VMEM((NZ, 2 * HALF, 128), BF16),
            pltpu.VMEM((2, 8, 4, NZ, HALF, 128), BF16),
            pltpu.VMEM((8, 16, 768), BF16),
            pltpu.VMEM((8, 16, 768), BF16),
            pltpu.VMEM((4, 16, 768), BF16),
            pltpu.VMEM((128, TILE), BF16),
            pltpu.VMEM((128, TILE), BF16),
            pltpu.VMEM((TILE, 256), BF16),
            pltpu.VMEM((own_cols // 128, 128), F32),
            pltpu.VMEM((80, TILE), F32),
            pltpu.VMEM((2, 4, half, 128), F32),
            *[pltpu.VMEM((2, 4, half, 128), BF16)] * 4,
            *[pltpu.VMEM((2, 4, half // 4, 128), BF16)] * 2,
            pltpu.VMEM((NZ, 16, 128), BF16),
            pltpu.VMEM((8, 16, 512), BF16),
            pltpu.VMEM((4, 16, 512), BF16),
            dma((3, 4)), dma((3, 4)), dma((NZ,)), dma((NZ,)), dma((2, 4)), dma((2, 4)),
            dma((2, 4)), dma((2, 8)), dma((2, 4)),
            *[dma((2, 4))] * 6,
            dma((NZ,)), dma((NZ,)), dma((3, 4)), dma((3, 4)),
        ],
        compiler_params=pltpu.CompilerParams(
            collective_id=0, has_side_effects=True, vmem_limit_bytes=63 * 2**20),
        name="evidence_gradients",
    )(*args)
    grad_rows, grad_cols = pl.pallas_call(
        functools.partial(unpack, 1.0 / points**0.5),
        out_shape=(
            jax.ShapeDtypeStruct((own_rows, FEAT), F32),
            jax.ShapeDtypeStruct((FEAT // row_size, own_cols), F32),
        ),
        in_specs=[vmem] * 2,
        out_specs=(vmem, vmem),
        name="unpack_gradients",
    )(*totals)
    return grad_rows.T, grad_cols


def solution(mesh):
    in_specs = (
        P(None, ("row", "col")),
        P(("row", "col")),
        P(None, ("row", "col")),
        P("row", "col"),
        P("col"),
        P("col"),
        P("row", "col"),
    )
    out_specs = (P(None, ("row", "col")), P("row", "col"))
    return jax.shard_map(body, mesh=mesh, in_specs=in_specs, out_specs=out_specs, check_vma=False)
```
